32 devices in a mesh: vocab: 16 (over z, y, x), rows: 2 (over core).
Axes of the slice: x: 2, y: 2, z: 4, core: 2. Of those that a mesh axis runs over, the one named last changes fastest.
Arguments:
- hidden: bfloat16 [1024, 4096], P('rows', 'vocab'), may hold values from -48 to 48
- head_weight: bfloat16 [4096, 16384], P('rows', 'vocab'), may hold values from -1 to 1
- in_proj: bfloat16 [4096, 64], replicated, may hold values from -0.09375 to 0.09375
- out_proj: bfloat16 [16384, 64], P('vocab'), may hold values from -6 to 6
- targets: int32 [1024], P('rows'), may hold values from 0 to 16383
- lengths: int32 [8], replicated, may hold values from 1 to 128, as said below
- grad_store: bfloat16 [8192, 4096], P(('vocab', 'rows')), may hold values from -0.09375 to 0.09375
Outputs:
- scores: float32 [8, 8192], P(None, ('vocab', 'rows'))
The draws below stay inside these ranges and needn't reach their ends.
Inputs may be any that keep to these rules, and one draw needn't show every extreme that they name: `lengths`: at least one sequence has exactly 128 valid rows.
All inputs are finite; a program needn't handle non-finite values.
Results may differ from the reference program's by a relative error of at most 0.0029.
Values may be sent and summed in bfloat16 or wider, within the bound.
A program may use at most 64 MiB of HBM per device.

```python
import math
import jax
import jax.numpy as jnp
from jax import lax

D = 4096
VOCAB = 16384
K = 64
TILE = 128
TOKENS = 1024
NSEQ = 8
NSTORE = 8192


def head_column(head_key, column):
    values = jax.random.normal(jax.random.fold_in(head_key, column), (D,), jnp.float32)
    return jnp.clip(values, -6.0, 6.0) / math.sqrt(D)


def draw_head_weight(key, part):
    head_key = jax.random.fold_in(key, 11)
    columns = jax.vmap(lambda column: head_column(head_key, column))(jnp.arange(VOCAB, dtype=jnp.int32))
    return columns.T.astype(jnp.bfloat16)


def draw_hidden(key, part):
    base_key = jax.random.fold_in(key, 12)
    values = jnp.clip(jax.random.normal(base_key, (TOKENS, D), jnp.float32), -6.0, 6.0)
    return jnp.clip(values, -48.0, 48.0).astype(jnp.bfloat16)


def draw_lengths(key, part):
    drawn = jax.random.randint(jax.random.fold_in(key, 13), (NSEQ,), 1, TILE + 1)
    longest = jax.random.randint(jax.random.fold_in(key, 14), (), 0, NSEQ)
    return drawn.at[longest].set(TILE).astype(jnp.int32)


def touch_ends(values, own_key, least, largest):
    dims = values.shape
    index_at = [jax.random.randint(jax.random.fold_in(own_key, axis), (), 0, dims[axis]) for axis in range(len(dims))]
    values = values.at[tuple(index_at)].set(least)
    longest = dims.index(max(dims))
    index_at[longest] = (index_at[longest] + 1) % dims[longest]
    return values.at[tuple(index_at)].set(largest)


def steps_of(rng, dims, cuts, least, top_value):
    level, own = 1.0, jax.random.fold_in(rng, 6)
    for axis_at, shards_of in cuts:
        draws = jnp.exp(jax.random.uniform(jax.random.fold_in(own, axis_at), (shards_of,), jnp.float32, least / len(cuts), top_value / len(cuts)))
        level = level * jnp.repeat(draws, dims[axis_at] // shards_of).reshape([-1 if axis == axis_at else 1 for axis in range(len(dims))])
    return level


def scatter_about(key, extent, spread, most, pieces=(), kind=jnp.bfloat16):
    values = jax.random.normal(key, extent, jnp.float32) * spread
    if len(pieces) > 0:
        values = steps_of(key, extent, pieces, -0.22, 0.18) * values
    return jnp.clip(values, min=-most, max=most).astype(kind)


def setup_inputs(seed: int = 0) -> dict:
    key_list = jax.random.split(jax.random.key(seed), 8)
    hidden = draw_hidden(jax.random.fold_in(key_list[7], 71), 0)
    head_weight = draw_head_weight(jax.random.fold_in(key_list[7], 71), 0)
    in_proj = scatter_about(key_list[2], (D, K), D ** -0.5, 0.09375)
    out_proj = scatter_about(key_list[3], (VOCAB, K), 1.0, 6.0, ((0, 16),))
    targets = touch_ends(jax.random.randint(key_list[4], (TOKENS,), 0, VOCAB), jax.random.fold_in(key_list[4], 1), 0, VOCAB - 1).astype(jnp.int32)
    lengths = draw_lengths(jax.random.fold_in(key_list[7], 71), 0)
    grad_store = scatter_about(key_list[6], (NSTORE, K * K), (K * K) ** -0.5, 0.09375, ((0, 32),))
    return {"hidden": hidden, "head_weight": head_weight, "in_proj": in_proj, "out_proj": out_proj, "targets": targets, "lengths": lengths, "grad_store": grad_store}


damping_ratio = 0.1
tiny_value = 1e-06

def whiten(seq_grads, cov_out, cov_in):
    proj_width = cov_out.shape[0]
    seq_count = seq_grads.shape[0]
    identity = jnp.eye(proj_width, dtype=jnp.float32)
    damp_out = damping_ratio * jnp.trace(cov_out) / proj_width + tiny_value
    damp_in = damping_ratio * jnp.trace(cov_in) / proj_width + tiny_value
    lower_out = jnp.linalg.cholesky(cov_out + damp_out * identity)
    lower_in = jnp.linalg.cholesky(cov_in + damp_in * identity)
    stacked = jnp.transpose(seq_grads, (1, 0, 2)).reshape(proj_width, seq_count * proj_width)
    left_half = lax.linalg.triangular_solve(lower_out, stacked, left_side=True, lower=True)
    left_full = lax.linalg.triangular_solve(lower_out, left_half, left_side=True, lower=True, transpose_a=True)
    rows_form = jnp.transpose(left_full.reshape(proj_width, seq_count, proj_width), (1, 0, 2)).reshape(seq_count * proj_width, proj_width)
    right_half = lax.linalg.triangular_solve(lower_in, rows_form, left_side=False, lower=True, transpose_a=True)
    right_full = lax.linalg.triangular_solve(lower_in, right_half, left_side=False, lower=True)
    return right_full.reshape(seq_count, proj_width * proj_width)

def reference(hidden, head_weight, in_proj, out_proj, targets, lengths, grad_store):
    vocab_size = head_weight.shape[1]
    proj_width = in_proj.shape[1]
    seq_count = lengths.shape[0]
    out_table = out_proj.astype(jnp.float32)
    columns = jnp.arange(vocab_size, dtype=jnp.int32)

    def tile_grad(inputs):
        tile_rows, tile_targets = inputs
        logits = jnp.dot(tile_rows.astype(jnp.float32), head_weight.astype(jnp.float32), preferred_element_type=jnp.float32)
        row_max = lax.optimization_barrier(jnp.max(logits, axis=1, keepdims=True))
        exponent = jnp.exp(logits - row_max)
        probability = exponent / lax.optimization_barrier(jnp.sum(exponent, axis=1, keepdims=True))
        onehot = (columns[None, :] == tile_targets[:, None]).astype(jnp.float32)
        return jnp.dot(probability - onehot, out_table, precision=lax.Precision.HIGHEST)
    out_grad = lax.map(tile_grad, (hidden.reshape(seq_count, TILE, -1), targets.reshape(seq_count, TILE)))
    input_proj = jnp.dot(hidden.astype(jnp.float32), in_proj.astype(jnp.float32), preferred_element_type=jnp.float32).reshape(seq_count, TILE, proj_width)
    position = jnp.arange(TILE, dtype=jnp.int32)
    is_valid = (position[None, :] < lengths[:, None]).astype(jnp.float32)[:, :, None]
    out_grad = out_grad * is_valid
    input_proj = input_proj * is_valid
    row_total = jnp.sum(lengths).astype(jnp.float32)
    flat_out = out_grad.reshape(-1, proj_width)
    flat_in = input_proj.reshape(-1, proj_width)
    cov_out = jnp.dot(flat_out.T, flat_out, precision=lax.Precision.HIGHEST) / row_total
    cov_in = jnp.dot(flat_in.T, flat_in, precision=lax.Precision.HIGHEST) / row_total
    seq_grads = jnp.einsum('stk,stj->skj', out_grad, input_proj, precision=lax.Precision.HIGHEST)
    seq_grads = seq_grads / jnp.sqrt(lengths.astype(jnp.float32))[:, None, None]
    whitened = whiten(seq_grads, cov_out, cov_in).astype(jnp.bfloat16)
    return jnp.dot(whitened.astype(jnp.float32), grad_store.T.astype(jnp.float32), preferred_element_type=jnp.float32)
```

```python
import functools

import jax
import jax.numpy as jnp
from jax import lax
from jax.experimental import pallas as pl
from jax.experimental.pallas import tpu as pltpu
from jax.sharding import PartitionSpec as P

TILE = 128


damping_ratio = 0.1
tiny_value = 1e-06


def joined(value, axis, join):
    pieces = jax.tree.map(lambda part: lax.all_gather(part, axis), value)
    head = jax.tree.map(lambda part: part[0], pieces)
    tail = jax.tree.map(lambda part: part[1:], pieces)
    running, _ = lax.scan(lambda running, slab: (join(running, slab), None), head, tail)
    return running


def whiten(seq_grads, cov_out, cov_in):
    proj_width = cov_out.shape[0]
    seq_count = seq_grads.shape[0]
    identity = jnp.eye(proj_width, dtype=jnp.float32)
    damp_out = damping_ratio * jnp.trace(cov_out) / proj_width + tiny_value
    damp_in = damping_ratio * jnp.trace(cov_in) / proj_width + tiny_value
    lower_out = jnp.linalg.cholesky(cov_out + damp_out * identity)
    lower_in = jnp.linalg.cholesky(cov_in + damp_in * identity)
    stacked = jnp.transpose(seq_grads, (1, 0, 2)).reshape(proj_width, seq_count * proj_width)
    left_half = lax.linalg.triangular_solve(lower_out, stacked, left_side=True, lower=True)
    left_full = lax.linalg.triangular_solve(
        lower_out, left_half, left_side=True, lower=True, transpose_a=True
    )
    rows_form = jnp.transpose(
        left_full.reshape(proj_width, seq_count, proj_width), (1, 0, 2)
    ).reshape(seq_count * proj_width, proj_width)
    right_half = lax.linalg.triangular_solve(
        lower_in, rows_form, left_side=False, lower=True, transpose_a=True
    )
    right_full = lax.linalg.triangular_solve(lower_in, right_half, left_side=False, lower=True)
    return right_full.reshape(seq_count, proj_width * proj_width)


def combine_rows(earlier, later):
    max_one, sum_one, weight_one = earlier
    max_two, sum_two, weight_two = later
    joint_max = jnp.maximum(max_one, max_two)
    scale_one = jnp.exp(max_one - joint_max)
    scale_two = jnp.exp(max_two - joint_max)
    joint_sum = sum_one * scale_one + sum_two * scale_two
    joint_weight = weight_one * scale_one[:, None] + weight_two * scale_two[:, None]
    return (joint_max, joint_sum, joint_weight)


def per_device(hidden, head_weight, in_proj, out_proj, targets, lengths, grad_store):
    token_count = hidden.shape[0]
    vocab_cols = head_weight.shape[1]
    proj_width = in_proj.shape[1]
    tile_count = token_count // TILE
    features = lax.all_gather(hidden, "vocab", axis=1, tiled=True)
    out_table = out_proj.astype(jnp.float32)
    first_column = lax.axis_index("vocab") * vocab_cols
    column_ids = lax.broadcasted_iota(jnp.int32, (token_count, vocab_cols), 1) + first_column
    onehot = (column_ids == targets[:, None]).astype(jnp.float32)
    picked_local = jnp.dot(onehot, out_table, precision=lax.Precision.HIGHEST)
    picked = lax.psum(picked_local, "vocab")
    logits = jnp.dot(
        features,
        lax.all_gather(head_weight, "rows", axis=0, tiled=True),
        preferred_element_type=jnp.float32,
    )
    local_max = jnp.max(logits, axis=1)
    exponent = jnp.exp(logits - local_max[:, None])
    weighted = jnp.dot(exponent, out_table, precision=lax.Precision.HIGHEST)
    merged = joined((local_max, jnp.sum(exponent, axis=1), weighted), "vocab", combine_rows)
    out_grad = merged[2] / merged[1][:, None] - picked
    input_proj = jnp.dot(features, in_proj, preferred_element_type=jnp.float32)
    own_lengths = lax.dynamic_slice_in_dim(lengths, lax.axis_index("rows") * tile_count, tile_count)
    position = lax.broadcasted_iota(jnp.int32, (tile_count, TILE), 1)
    is_valid = (position < own_lengths[:, None]).astype(jnp.float32)[:, :, None]
    out_tiles = out_grad.reshape(tile_count, TILE, proj_width) * is_valid
    in_tiles = input_proj.reshape(tile_count, TILE, proj_width) * is_valid
    flat_out = out_tiles.reshape(token_count, proj_width)
    flat_in = in_tiles.reshape(token_count, proj_width)
    local_out = jnp.dot(flat_out.T, flat_out, precision=lax.Precision.HIGHEST)
    local_in = jnp.dot(flat_in.T, flat_in, precision=lax.Precision.HIGHEST)
    cov_out, cov_in = lax.psum((local_out, local_in), "rows")
    row_total = jnp.sum(lengths).astype(jnp.float32)
    seq_grads = jnp.einsum("stk,stj->skj", out_tiles, in_tiles, precision=lax.Precision.HIGHEST)
    seq_grads = seq_grads / jnp.sqrt(own_lengths.astype(jnp.float32))[:, None, None]
    whitened = whiten(seq_grads, cov_out / row_total, cov_in / row_total).astype(jnp.bfloat16)
    return jnp.dot(
        lax.all_gather(whitened, "rows", axis=0, tiled=True),
        grad_store.T,
        preferred_element_type=jnp.float32,
    )


LANES = 128
HIGHEST = lax.Precision.HIGHEST
MESH = pl.DeviceIdType.MESH


def dot_f32(left, right, dims):
    return lax.dot_general(
        left, right, (dims, ((), ())), precision=HIGHEST, preferred_element_type=jnp.float32
    )


def kernel(
    line,
    parts,
    hidden_ref,
    head_ref,
    in_proj_ref,
    out_proj_ref,
    targets_ref,
    lengths_ref,
    store_ref,
    scores_ref,
    feat,
    weights,
    logits,
    inner,
    store,
    table,
    pick,
    pick_in,
    stat,
    stat_in,
    grad,
    grad_in,
    mix,
    mix_in,
    white,
    flat,
    load_sem,
    head_send,
    head_recv,
    feat_send,
    feat_recv,
    pick_sems,
    stat_sems,
    grad_sems,
    mix_send,
    mix_recv,
):
    count = line * 4
    me = lax.axis_index("vocab")
    row = lax.axis_index("rows")
    z, y, x = me // 4, (me // 2) % 2, me % 2
    tokens, block = hidden_ref.shape
    half = tokens // 2
    depth, vocab_cols = head_ref.shape
    width = out_proj_ref.shape[1]
    own = tokens // count
    tiles = tokens // TILE
    seq_count = tiles * parts

    def send(source, target, send_sem, recv_sem, device):
        return pltpu.make_async_remote_copy(
            src_ref=source,
            dst_ref=target,
            send_sem=send_sem,
            recv_sem=recv_sem,
            device_id=device,
            device_id_type=MESH,
        )

    def await_bytes(ref, sem):
        pltpu.make_async_copy(ref, ref, sem).wait()

    barrier = pltpu.get_barrier_semaphore()

    def greet(step, carry):
        pl.semaphore_signal(
            barrier, inc=1, device_id={"vocab": (me + step) % count}, device_id_type=MESH
        )
        return carry

    lax.fori_loop(1, count, greet, 0)
    for step in range(1, parts):
        pl.semaphore_signal(
            barrier, inc=1, device_id={"rows": (row + step) % parts}, device_id_type=MESH
        )
    own_rows = pl.ds(pl.multiple_of(row * depth, depth), depth)
    local_feat = pltpu.make_async_copy(hidden_ref, feat.at[me], load_sem.at[0])
    local_head = pltpu.make_async_copy(head_ref, weights.at[own_rows], load_sem.at[1])
    local_store = pltpu.make_async_copy(store_ref, store, load_sem.at[2])
    local_feat.start()
    local_head.start()
    local_store.start()
    pl.semaphore_wait(barrier, count - 1 + parts - 1)

    def place(zz, yy, xx):
        return (zz * 2 + yy) * 2 + xx

    def item(zz, side, pair):
        flips = {0: (0, 0), 1: (0, 1), 2: (1, 0), 3: (1, 1)}[pair if side == 0 else (0, 2, 1, 3)[pair]]
        return place(zz, (y + flips[0]) % 2, (x + flips[1]) % 2)

    def piece(index, side):
        return feat.at[index, pl.ds(side * half, half)]

    def hop(index, side, route, device, source=None):
        return send(
            piece(index, side) if source is None else source,
            piece(index, side),
            feat_send.at[route, side, index],
            feat_recv.at[side, index],
            {"vocab": device},
        )

    nearest = jnp.minimum(z, line - 1 - z)

    def nth(k):
        if k == 0:
            return z
        sign_near = -1 if k % 2 == 1 else 1
        sign_far = jnp.where(z < line - 1 - z, 1, -1)
        return z + jnp.where(k <= 2 * nearest, sign_near * ((k + 1) // 2), sign_far * (k - nearest))

    def outward(k, side, action):
        zz = nth(k)
        index = place(zz, y, x)
        source = hidden_ref.at[pl.ds(side * half, half)] if k == 0 else None
        up = jnp.logical_and(zz <= z, z < line - 1)
        down = jnp.logical_and(zz >= z, z > 0)
        if k > 0:
            up = jnp.logical_and(zz < z, z < line - 1)
            down = jnp.logical_and(zz > z, z > 0)

        @pl.when(up)
        def _():
            action(hop(index, side, 0, place(jnp.minimum(z + 1, line - 1), y, x), source))

        @pl.when(down)
        def _():
            action(hop(index, side, 1, place(jnp.maximum(z - 1, 0), y, x), source))

        action(hop(index, side, 2, item(z, side, 1), source))
        action(hop(index, side, 3, item(z, side, 2), source))

    def onward(k, side):
        return hop(item(nth(k), side, 1), side, 2, item(z, side, 2))

    def arrived(index, side):
        hop(index, side, 0, me).wait_recv()

    def multiply(k):
        zz = nth(k)

        def body(step, carry):
            side, pair = step % 2, step // 2
            near, far = pair % 2, pair // 2
            flip_x = (1 - side) * near + side * far
            flip_y = (1 - side) * far + side * near
            index = place(zz, (y + flip_y) % 2, (x + flip_x) % 2)

            @pl.when(pair >= 2)
            def _():
                arrived(index, side)

            rows = pl.ds(pl.multiple_of(side * half, half), half)
            columns = pl.ds(pl.multiple_of(index * block, block), block)
            features = feat[index, rows, :]
            logits[rows, :] += jnp.dot(
                features, weights[columns, :], preferred_element_type=jnp.float32
            )
            inner[rows, :] += jnp.dot(
                features, in_proj_ref[columns, :], preferred_element_type=jnp.float32
            )
            return carry

        lax.fori_loop(0, 8, body, 0)

    for side in range(2):
        outward(0, side, lambda copy: copy.start())
    head_copies = []
    for step in range(1, parts):
        copy = send(
            head_ref,
            weights.at[own_rows],
            head_send.at[step],
            head_recv.at[row],
            {"rows": (row + step) % parts},
        )
        copy.start()
        head_copies.append(copy)

    lane = lax.broadcasted_iota(jnp.int32, (vocab_cols, LANES - width), 1)
    table[:, :width] = out_proj_ref[...]
    table[:, width:] = (lane == 0).astype(jnp.float32).astype(jnp.bfloat16)
    column_ids = lax.broadcasted_iota(jnp.int32, (vocab_cols, tokens), 0) + me * vocab_cols
    onehot = (column_ids == targets_ref[...]).astype(jnp.float32).astype(jnp.bfloat16)
    pick[...] = lax.dot_general(
        onehot, table[...], (((0,), (0,)), ((), ())), preferred_element_type=jnp.float32
    ).astype(jnp.bfloat16)

    def own_part(ref, device):
        return ref.at[pl.ds(pl.multiple_of(device * own, own), own)]

    def slot(device):
        return (me - device - 1 + 2 * count) % count

    def send_pick(step, carry):
        device = (me + step) % count
        send(
            own_part(pick, device),
            pick_in.at[slot(device)],
            pick_sems.at[0],
            pick_sems.at[1],
            {"vocab": device},
        ).start()
        return carry

    lax.fori_loop(1, count, send_pick, 0)
    logits[...] = jnp.zeros_like(logits)
    inner[...] = jnp.zeros_like(inner)

    for k in range(line):
        if k > 0:
            for side in range(2):
                arrived(place(nth(k), y, x), side)
                outward(k, side, lambda copy: copy.start())
            for side in range(2):
                arrived(item(nth(k - 1), side, 1), side)
                onward(k - 1, side).start()
        if k == 1:
            local_feat.wait()
            local_head.wait()
            for step in range(1, parts):
                other = (row + step) % parts
                rows = pl.ds(pl.multiple_of(other * depth, depth), depth)
                send(head_ref, weights.at[rows], head_send.at[0], head_recv.at[other], {"rows": row}).wait_recv()
        if k > 1:
            multiply(k - 2)
    for side in range(2):
        arrived(item(nth(line - 1), side, 1), side)
        onward(line - 1, side).start()
    multiply(line - 2)
    multiply(line - 1)

    lanes = lax.broadcasted_iota(jnp.int32, (TILE, LANES), 1)
    per_tile = TILE // own
    for tile in range(tiles):
        part = logits[tile * TILE : (tile + 1) * TILE, :]
        top = jnp.max(part, axis=1, keepdims=True)
        exponent = jnp.exp(part - top)
        upper = exponent.astype(jnp.bfloat16)
        lower = (exponent - upper.astype(jnp.float32)).astype(jnp.bfloat16)
        weighted = jnp.dot(upper, table[...], preferred_element_type=jnp.float32) + jnp.dot(
            lower, table[...], preferred_element_type=jnp.float32
        )
        stat[tile * TILE : (tile + 1) * TILE, :] = jnp.where(lanes == width + 1, top, weighted)
        for device in range(tile * per_tile, (tile + 1) * per_tile):

            @pl.when(me != device)
            def _():
                send(
                    stat.at[pl.ds(device * own, own)],
                    stat_in.at[slot(device)],
                    stat_sems.at[0],
                    stat_sems.at[1],
                    {"vocab": device},
                ).start()

    position = lax.broadcasted_iota(jnp.int32, (TILE, LANES), 0)
    masked_in = []
    for tile in range(tiles):
        valid = (position < lengths_ref[row * tiles + tile]).astype(jnp.float32)
        masked_in.append(inner[tile * TILE : (tile + 1) * TILE, :] * valid[:, :width])
    flat_in = jnp.concatenate(masked_in, axis=0)
    padded_in = jnp.concatenate([jnp.zeros_like(flat_in), flat_in], axis=1)
    mix[row, tiles] = dot_f32(flat_in, padded_in, ((0,), (0,)))

    await_bytes(pick_in, pick_sems.at[1])
    picked = own_part(pick, me)[...].astype(jnp.float32)
    for other in range(count - 1):
        picked = picked + pick_in[other].astype(jnp.float32)
    await_bytes(stat_in, stat_sems.at[1])
    mine = own_part(stat, me)[...]
    tops = [mine[:, width + 1 : width + 2]]
    for other in range(count - 1):
        tops.append(stat_in[other][:, width + 1 : width + 2])
    joint = functools.reduce(jnp.maximum, tops)
    total = mine * jnp.exp(tops[0] - joint)
    for other in range(count - 1):
        total = total + stat_in[other] * jnp.exp(tops[other + 1] - joint)
    first = me * own
    place_in_tile = lax.broadcasted_iota(jnp.int32, (own, LANES), 0) + first % TILE
    valid = (place_in_tile < lengths_ref[row * tiles + first // TILE]).astype(jnp.float32)
    finished = (total / total[:, width : width + 1] - picked) * valid
    grad[...] = jnp.concatenate([finished[: own // 2, :width], finished[own // 2 :, :width]], axis=1)

    def send_grad(step, carry):
        device = (me + step) % count
        send(grad, grad_in.at[me], grad_sems.at[0], grad_sems.at[1], {"vocab": device}).start()
        return carry

    lax.fori_loop(1, count, send_grad, 0)
    grad_in[me] = grad[...]
    await_bytes(grad_in.at[pl.ds(0, count - 1)], grad_sems.at[1])

    for tile in range(tiles):
        pieces = []
        for other in range(tile * per_tile, (tile + 1) * per_tile):
            pieces += [grad_in[other][:, :width], grad_in[other][:, width:]]
        grads = jnp.concatenate(pieces, axis=0)
        joined_sides = jnp.concatenate([grads, masked_in[tile]], axis=1)
        mix[row, tile] = dot_f32(grads, joined_sides, ((0,), (0,)))
    mix_copies = []
    for step in range(1, parts):
        copy = send(
            mix.at[row], mix_in.at[row], mix_send.at[step], mix_recv.at[row], {"rows": (row + step) % parts}
        )
        copy.start()
        mix_copies.append(copy)
    mix_in[row] = mix[row]
    for step in range(1, parts):
        other = (row + step) % parts
        send(mix.at[row], mix_in.at[other], mix_send.at[0], mix_recv.at[other], {"rows": row}).wait_recv()

    row_total = lengths_ref[0]
    for sequence in range(1, seq_count):
        row_total = row_total + lengths_ref[sequence]
    one_over = 1.0 / jnp.full((1, LANES), row_total, jnp.int32).astype(jnp.float32)
    cov_out = jnp.zeros((width, LANES), jnp.float32)
    cov_in = jnp.zeros((width, LANES), jnp.float32)
    for part in range(parts):
        for tile in range(tiles):
            cov_out = cov_out + mix_in[part, tile]
        cov_in = cov_in + mix_in[part, tiles]
    left = lax.broadcasted_iota(jnp.int32, (width, LANES), 1) < width
    cov = jnp.concatenate([jnp.where(left, cov_out, 0.0), cov_in], axis=0) * one_over
    identity = (
        lax.broadcasted_iota(jnp.int32, (LANES, LANES), 0)
        == lax.broadcasted_iota(jnp.int32, (LANES, LANES), 1)
    ).astype(jnp.float32)
    diagonal = jnp.sum(cov * identity, axis=0, keepdims=True)
    left_row = lax.broadcasted_iota(jnp.int32, (1, LANES), 1) < width
    trace_out = jnp.sum(jnp.where(left_row, diagonal, 0.0), axis=1, keepdims=True)
    trace_in = jnp.sum(jnp.where(left_row, 0.0, diagonal), axis=1, keepdims=True)
    trace = jnp.where(left_row, trace_out, trace_in)
    damp = damping_ratio * trace / width + tiny_value
    middle = damp + 0.5 * trace
    scaled = (cov + identity * damp) * (1.0 / middle)
    reach = 1.0 / (1.0 + 2.0 * damping_ratio / width)
    gain = 2.0 / (2.0 - reach * reach)
    inverse = gain * (2.0 * identity - scaled)
    reach = reach * reach / (2.0 - reach * reach)
    while reach > 1e-8:
        gain = 2.0 / (2.0 - reach * reach)
        again = dot_f32(scaled, inverse, ((1,), (0,)))
        inverse = gain * (2.0 * inverse - dot_f32(inverse, again, ((1,), (0,))))
        reach = reach * reach / (2.0 - reach * reach)
    inverse = inverse * (1.0 / middle)
    stacked = []
    for part in range(parts):
        for tile in range(tiles):
            long = jnp.full((1, LANES), lengths_ref[part * tiles + tile], jnp.int32)
            stacked.append(mix_in[part, tile] * lax.rsqrt(long.astype(jnp.float32)))
    right = dot_f32(jnp.concatenate(stacked, axis=0), inverse, ((1,), (0,)))
    corner = inverse[:width, :width]
    for sequence in range(seq_count):
        rows = slice(sequence * width, (sequence + 1) * width)
        white[rows, :] = dot_f32(corner, right[rows, :], ((1,), (0,)))
    for pair in range(width // 2):
        even = white[pl.ds(2 * pair, seq_count, stride=width), :]
        odd = white[pl.ds(2 * pair + 1, seq_count, stride=width), :]
        flat[:, pair * LANES : (pair + 1) * LANES] = jnp.concatenate(
            [even[:, width:], odd[:, width:]], axis=1
        )
    local_store.wait()
    scores_ref[...] = lax.dot_general(
        flat[...].astype(jnp.bfloat16),
        store[...],
        (((1,), (1,)), ((), ())),
        preferred_element_type=jnp.float32,
    )

    for k in range(line):
        for side in range(2):
            outward(k, side, lambda copy: copy.wait_send())
            onward(k, side).wait_send()
    for copy in head_copies + mix_copies:
        copy.wait_send()
    await_bytes(pick_in, pick_sems.at[0])
    await_bytes(stat_in, stat_sems.at[0])
    await_bytes(grad_in.at[pl.ds(0, count - 1)], grad_sems.at[0])


def per_device_any(count, parts, hidden, head_weight, in_proj, out_proj, targets, lengths, grad_store):
    tokens, block = hidden.shape
    vocab_cols = head_weight.shape[1]
    width = in_proj.shape[1]
    own = tokens // count
    tiles = tokens // TILE
    fits = (
        count % 4 == 0
        and block % LANES == 0
        and 2 * width == LANES
        and own % 32 == 0
        and TILE % own == 0
        and grad_store.shape[1] == width * width
    )
    if not fits:
        return per_device(hidden, head_weight, in_proj, out_proj, targets, lengths, grad_store)
    line = count // 4
    seq_count = lengths.shape[0]
    anywhere = pl.BlockSpec(memory_space=pl.ANY)
    vmem = pl.BlockSpec(memory_space=pltpu.VMEM)
    smem = pl.BlockSpec(memory_space=pltpu.SMEM)
    dma = pltpu.SemaphoreType.DMA
    f32, bf16 = jnp.float32, jnp.bfloat16
    return pl.pallas_call(
        functools.partial(kernel, line, parts),
        out_shape=jax.ShapeDtypeStruct((seq_count, grad_store.shape[0]), f32),
        in_specs=[anywhere, anywhere, vmem, vmem, vmem, smem, anywhere],
        out_specs=vmem,
        scratch_shapes=[
            pltpu.VMEM((count, tokens, block), bf16),
            pltpu.VMEM((head_weight.shape[0] * parts, vocab_cols), bf16),
            pltpu.VMEM((tokens, vocab_cols), f32),
            pltpu.VMEM((tokens, width), f32),
            pltpu.VMEM(grad_store.shape, bf16),
            pltpu.VMEM((vocab_cols, LANES), bf16),
            pltpu.VMEM((tokens, LANES), bf16),
            pltpu.VMEM((count - 1, own, LANES), bf16),
            pltpu.VMEM((tokens, LANES), f32),
            pltpu.VMEM((count - 1, own, LANES), f32),
            pltpu.VMEM((own // 2, LANES), f32),
            pltpu.VMEM((count, own // 2, LANES), f32),
            pltpu.VMEM((parts, tiles + 1, width, LANES), f32),
            pltpu.VMEM((parts, tiles + 1, width, LANES), f32),
            pltpu.VMEM((seq_count * width, LANES), f32),
            pltpu.VMEM((seq_count, width * width), f32),
            dma((3,)),
            dma((parts,)),
            dma((parts,)),
            dma((4, 2, count)),
            dma((2, count)),
            dma((2,)),
            dma((2,)),
            dma((2,)),
            dma((parts,)),
            dma((parts,)),
        ],
        compiler_params=pltpu.CompilerParams(
            collective_id=0, has_side_effects=True, vmem_limit_bytes=48 * 1024 * 1024
        ),
        cost_estimate=pl.CostEstimate(
            flops=2 * tokens * block * count * vocab_cols,
            bytes_accessed=4 * tokens * block * count,
            transcendentals=tokens * vocab_cols,
        ),
    )(hidden, head_weight, in_proj, out_proj, targets[None, :], lengths, grad_store)


def solution(mesh):
    return jax.shard_map(
        functools.partial(per_device_any, mesh.shape["vocab"], mesh.shape["rows"]),
        mesh=mesh,
        in_specs=(
            P("rows", "vocab"),
            P("rows", "vocab"),
            P(),
            P("vocab", None),
            P("rows"),
            P(),
            P(("vocab", "rows"), None),
        ),
        out_specs=P(None, ("vocab", "rows")),
        check_vma=False,
    )
```

```python
import functools

import jax
import jax.numpy as jnp
from jax import lax
from jax.experimental import pallas as pl
from jax.experimental.pallas import tpu as pltpu
from jax.sharding import PartitionSpec as P

TILE = 128


damping_ratio = 0.1
tiny_value = 1e-06


def joined(value, axis, join):
    pieces = jax.tree.map(lambda part: lax.all_gather(part, axis), value)
    head = jax.tree.map(lambda part: part[0], pieces)
    tail = jax.tree.map(lambda part: part[1:], pieces)
    running, _ = lax.scan(lambda running, slab: (join(running, slab), None), head, tail)
    return running


def whiten(seq_grads, cov_out, cov_in):
    proj_width = cov_out.shape[0]
    seq_count = seq_grads.shape[0]
    identity = jnp.eye(proj_width, dtype=jnp.float32)
    damp_out = damping_ratio * jnp.trace(cov_out) / proj_width + tiny_value
    damp_in = damping_ratio * jnp.trace(cov_in) / proj_width + tiny_value
    lower_out = jnp.linalg.cholesky(cov_out + damp_out * identity)
    lower_in = jnp.linalg.cholesky(cov_in + damp_in * identity)
    stacked = jnp.transpose(seq_grads, (1, 0, 2)).reshape(proj_width, seq_count * proj_width)
    left_half = lax.linalg.triangular_solve(lower_out, stacked, left_side=True, lower=True)
    left_full = lax.linalg.triangular_solve(
        lower_out, left_half, left_side=True, lower=True, transpose_a=True
    )
    rows_form = jnp.transpose(
        left_full.reshape(proj_width, seq_count, proj_width), (1, 0, 2)
    ).reshape(seq_count * proj_width, proj_width)
    right_half = lax.linalg.triangular_solve(
        lower_in, rows_form, left_side=False, lower=True, transpose_a=True
    )
    right_full = lax.linalg.triangular_solve(lower_in, right_half, left_side=False, lower=True)
    return right_full.reshape(seq_count, proj_width * proj_width)


def combine_rows(earlier, later):
    max_one, sum_one, weight_one = earlier
    max_two, sum_two, weight_two = later
    joint_max = jnp.maximum(max_one, max_two)
    scale_one = jnp.exp(max_one - joint_max)
    scale_two = jnp.exp(max_two - joint_max)
    joint_sum = sum_one * scale_one + sum_two * scale_two
    joint_weight = weight_one * scale_one[:, None] + weight_two * scale_two[:, None]
    return (joint_max, joint_sum, joint_weight)


def per_device(hidden, head_weight, in_proj, out_proj, targets, lengths, grad_store):
    token_count = hidden.shape[0]
    vocab_cols = head_weight.shape[1]
    proj_width = in_proj.shape[1]
    tile_count = token_count // TILE
    features = lax.all_gather(hidden, "vocab", axis=1, tiled=True)
    out_table = out_proj.astype(jnp.float32)
    first_column = lax.axis_index("vocab") * vocab_cols
    column_ids = lax.broadcasted_iota(jnp.int32, (token_count, vocab_cols), 1) + first_column
    onehot = (column_ids == targets[:, None]).astype(jnp.float32)
    picked_local = jnp.dot(onehot, out_table, precision=lax.Precision.HIGHEST)
    picked = lax.psum(picked_local, "vocab")
    logits = jnp.dot(
        features,
        lax.all_gather(head_weight, "rows", axis=0, tiled=True),
        preferred_element_type=jnp.float32,
    )
    local_max = jnp.max(logits, axis=1)
    exponent = jnp.exp(logits - local_max[:, None])
    weighted = jnp.dot(exponent, out_table, precision=lax.Precision.HIGHEST)
    merged = joined((local_max, jnp.sum(exponent, axis=1), weighted), "vocab", combine_rows)
    out_grad = merged[2] / merged[1][:, None] - picked
    input_proj = jnp.dot(features, in_proj, preferred_element_type=jnp.float32)
    own_lengths = lax.dynamic_slice_in_dim(lengths, lax.axis_index("rows") * tile_count, tile_count)
    position = lax.broadcasted_iota(jnp.int32, (tile_count, TILE), 1)
    is_valid = (position < own_lengths[:, None]).astype(jnp.float32)[:, :, None]
    out_tiles = out_grad.reshape(tile_count, TILE, proj_width) * is_valid
    in_tiles = input_proj.reshape(tile_count, TILE, proj_width) * is_valid
    flat_out = out_tiles.reshape(token_count, proj_width)
    flat_in = in_tiles.reshape(token_count, proj_width)
    local_out = jnp.dot(flat_out.T, flat_out, precision=lax.Precision.HIGHEST)
    local_in = jnp.dot(flat_in.T, flat_in, precision=lax.Precision.HIGHEST)
    cov_out, cov_in = lax.psum((local_out, local_in), "rows")
    row_total = jnp.sum(lengths).astype(jnp.float32)
    seq_grads = jnp.einsum("stk,stj->skj", out_tiles, in_tiles, precision=lax.Precision.HIGHEST)
    seq_grads = seq_grads / jnp.sqrt(own_lengths.astype(jnp.float32))[:, None, None]
    whitened = whiten(seq_grads, cov_out / row_total, cov_in / row_total).astype(jnp.bfloat16)
    return jnp.dot(
        lax.all_gather(whitened, "rows", axis=0, tiled=True),
        grad_store.T,
        preferred_element_type=jnp.float32,
    )


LANES = 128
HIGHEST = lax.Precision.HIGHEST
MESH = pl.DeviceIdType.MESH


def dot_f32(left, right, dims):
    return lax.dot_general(
        left, right, (dims, ((), ())), precision=HIGHEST, preferred_element_type=jnp.float32
    )


def split(value):
    upper = value.astype(jnp.bfloat16)
    return upper, (value - upper.astype(jnp.float32)).astype(jnp.bfloat16)


def dot_three(left, right):
    left_upper, left_lower = split(left)
    right_upper, right_lower = split(right)
    small = jnp.dot(left_upper, right_lower, preferred_element_type=jnp.float32) + jnp.dot(
        left_lower, right_upper, preferred_element_type=jnp.float32
    )
    return small + jnp.dot(left_upper, right_upper, preferred_element_type=jnp.float32)


def kernel(
    line,
    parts,
    hidden_ref,
    head_ref,
    in_proj_hbm,
    out_proj_hbm,
    targets_hbm,
    lengths_hbm,
    store_ref,
    scores_ref,
    feat,
    weights,
    logits,
    inner,
    store,
    in_proj_ref,
    out_proj_ref,
    targets_ref,
    lengths_ref,
    table,
    pick,
    pick_in,
    stat,
    stat_in,
    grad,
    grad_in,
    mix,
    mix_in,
    white,
    flat,
    load_sem,
    head_send,
    head_recv,
    feat_send,
    feat_recv,
    pick_sems,
    stat_sems,
    grad_sems,
    mix_send,
    mix_recv,
):
    count = line * 4
    me = lax.axis_index("vocab")
    row = lax.axis_index("rows")
    z, y, x = me // 4, (me // 2) % 2, me % 2
    tokens, block = hidden_ref.shape
    long_rows, short_rows = class_rows(tokens)
    starts = (0, long_rows, 2 * long_rows, 2 * long_rows + short_rows)
    sizes = (long_rows, long_rows, short_rows, short_rows)
    depth, vocab_cols = head_ref.shape
    width = out_proj_ref.shape[0]
    own = tokens // count
    tiles = tokens // TILE
    seq_count = tiles * parts

    def send(source, target, send_sem, recv_sem, device):
        return pltpu.make_async_remote_copy(
            src_ref=source,
            dst_ref=target,
            send_sem=send_sem,
            recv_sem=recv_sem,
            device_id=device,
            device_id_type=MESH,
        )

    def await_bytes(ref, sem):
        pltpu.make_async_copy(ref, ref, sem).wait()

    barrier = pltpu.get_barrier_semaphore()

    def greet(step, carry):
        pl.semaphore_signal(
            barrier, inc=1, device_id={"vocab": (me + step) % count}, device_id_type=MESH
        )
        return carry

    lax.fori_loop(1, count, greet, 0)
    for step in range(1, parts):
        pl.semaphore_signal(
            barrier, inc=1, device_id={"rows": (row + step) % parts}, device_id_type=MESH
        )
    own_rows = pl.ds(pl.multiple_of(row * depth, depth), depth)
    local_feat = pltpu.make_async_copy(hidden_ref, feat.at[me], load_sem.at[0])
    local_head = pltpu.make_async_copy(head_ref, weights.at[own_rows], load_sem.at[1])
    local_store = pltpu.make_async_copy(store_ref, store, load_sem.at[2])
    local_feat.start()
    small = [
        pltpu.make_async_copy(source, target, load_sem.at[3 + at])
        for at, (source, target) in enumerate(
            [
                (out_proj_hbm, out_proj_ref),
                (targets_hbm, targets_ref),
                (lengths_hbm, lengths_ref),
                (in_proj_hbm, in_proj_ref),
            ]
        )
    ]
    for copy in small:
        copy.start()
    local_head.start()
    local_store.start()
    pl.semaphore_wait(barrier, count - 1 + parts - 1)

    def place(zz, yy, xx):
        return (zz * 2 + yy) * 2 + xx

    def item(zz, side, pair):
        near, far = pair % 2, pair // 2
        flip_y, flip_x = (far, near) if side % 2 == 0 else (near, far)
        return place(zz, (y + flip_y) % 2, (x + flip_x) % 2)

    def piece(index, side):
        return feat.at[index, pl.ds(starts[side], sizes[side])]

    def hop(index, side, route, device, source=None):
        return send(
            piece(index, side) if source is None else source,
            piece(index, side),
            feat_send.at[route, side, index],
            feat_recv.at[side, index],
            {"vocab": device},
        )

    nearest = jnp.minimum(z, line - 1 - z)

    def nth(k):
        if k == 0:
            return z
        sign_near = -1 if k % 2 == 1 else 1
        sign_far = jnp.where(z < line - 1 - z, 1, -1)
        return z + jnp.where(k <= 2 * nearest, sign_near * ((k + 1) // 2), sign_far * (k - nearest))

    def own_rows_of(side):
        return hidden_ref.at[pl.ds(starts[side], sizes[side])]

    def along(k, side, pair, action, source=None):
        zz = nth(k)
        index = item(zz, side, pair)
        up = z < line - 1
        down = z > 0
        if k > 0:
            up = jnp.logical_and(zz < z, up)
            down = jnp.logical_and(zz > z, down)

        @pl.when(up)
        def _():
            action(hop(index, side, 0, place(jnp.minimum(z + 1, line - 1), y, x), source))

        @pl.when(down)
        def _():
            action(hop(index, side, 1, place(jnp.maximum(z - 1, 0), y, x), source))

    def outward(k, side, action):
        source = own_rows_of(side) if k == 0 else None
        index = item(nth(k), side, 0)
        along(k, side, 0, action, source)
        action(hop(index, side, 2, item(z, side, 1), source))
        action(hop(index, side, 3, item(z, side, 2), source))

    def onward(k, side):
        return hop(item(nth(k), side, 1), side, 2, item(z, side, 2))

    def arrived(index, side):
        hop(index, side, 0, me).wait_recv()

    def accumulate(index, start, size):
        rows = pl.ds(pl.multiple_of(start, 16), size)
        columns = pl.ds(pl.multiple_of(index * block, block), block)
        features = feat[index, rows, :]
        logits[rows, :] += jnp.dot(
            features, weights[columns, :], preferred_element_type=jnp.float32
        )
        inner[rows, :] += lax.dot_general(
            features,
            in_proj_ref[:, columns],
            (((1,), (1,)), ((), ())),
            preferred_element_type=jnp.float32,
        )

    def multiply(k):
        zz = nth(k)

        def body(step, carry):
            side, pair = step % 2, step // 2
            near, far = pair % 2, pair // 2
            flip_x = (1 - side) * near + side * far
            flip_y = (1 - side) * far + side * near
            index = place(zz, (y + flip_y) % 2, (x + flip_x) % 2)

            @pl.when(pair >= 2)
            def _():
                pltpu.make_async_copy(
                    piece(index, 0), piece(index, 0), feat_recv.at[side, index]
                ).wait()

            accumulate(index, side * long_rows, long_rows)
            return carry

        lax.fori_loop(0, 8, body, 0)

    def multiply_short(k):
        zz = nth(k)

        def body(pair, carry):
            index = place(zz, (y + pair // 2) % 2, (x + pair % 2) % 2)
            accumulate(index, 2 * long_rows, 2 * short_rows)
            return carry

        lax.fori_loop(0, 4, body, 0)

    def short_arrivals(k):
        for pair in range(4):
            for side in (2, 3):
                if k > 0:
                    arrived(item(nth(k), side, pair), side)
                    along(k, side, pair, lambda copy: copy.start())

    def short_start(side, action):
        source = own_rows_of(side)
        action(hop(me, side, 2, item(z, side, 1), source))
        action(hop(me, side, 3, item(z, side, 2), source))
        along(0, side, 0, action, source)

    def short_onward(pair, side, action):
        index = item(z, side, pair)
        if pair == 1:
            action(hop(index, side, 2, item(z, side, 2)))
        along(0, side, pair, action)

    for side in (2, 3):
        short_start(side, lambda copy: copy.start())
    for side in range(2):
        outward(0, side, lambda copy: copy.start())
    head_copies = []
    for step in range(1, parts):
        copy = send(
            head_ref,
            weights.at[own_rows],
            head_send.at[step],
            head_recv.at[row],
            {"rows": (row + step) % parts},
        )
        copy.start()
        head_copies.append(copy)

    for copy in small:
        copy.wait()
    marker = lax.broadcasted_iota(jnp.int32, (LANES - width, vocab_cols), 0)
    upright = jnp.concatenate([out_proj_ref[...].astype(jnp.float32), (marker == 0).astype(jnp.float32)], axis=0)
    table[...] = upright.T.astype(jnp.bfloat16)
    column_ids = lax.broadcasted_iota(jnp.int32, (vocab_cols, tokens), 0) + me * vocab_cols
    onehot = (column_ids == targets_ref[...]).astype(jnp.float32).astype(jnp.bfloat16)
    pick[...] = jnp.dot(
        upright.astype(jnp.bfloat16), onehot, preferred_element_type=jnp.float32
    ).T.astype(jnp.bfloat16)

    def own_part(ref, device):
        return ref.at[pl.ds(pl.multiple_of(device * own, own), own)]

    def slot(device):
        return (me - device - 1 + 2 * count) % count

    def send_pick(step, carry):
        device = (me + step) % count
        send(
            own_part(pick, device),
            pick_in.at[slot(device)],
            pick_sems.at[0],
            pick_sems.at[1],
            {"vocab": device},
        ).start()
        return carry

    lax.fori_loop(1, count, send_pick, 0)
    logits[...] = jnp.zeros_like(logits)
    inner[...] = jnp.zeros_like(inner)

    for k in range(line):
        if k == 1:
            for pair in (1, 2, 3):
                for side in (2, 3):
                    arrived(item(z, side, pair), side)
                    short_onward(pair, side, lambda copy: copy.start())
        if k > 0:
            for side in range(2):
                arrived(place(nth(k), y, x), side)
                outward(k, side, lambda copy: copy.start())
            for side in range(2):
                arrived(item(nth(k - 1), side, 1), side)
                onward(k - 1, side).start()
            short_arrivals(k - 1)
        if k == 1:
            local_feat.wait()
            local_head.wait()
            for step in range(1, parts):
                other = (row + step) % parts
                rows = pl.ds(pl.multiple_of(other * depth, depth), depth)
                send(head_ref, weights.at[rows], head_send.at[0], head_recv.at[other], {"rows": row}).wait_recv()
        if k > 1:
            multiply(k - 2)
            multiply_short(k - 2)
    for side in range(2):
        arrived(item(nth(line - 1), side, 1), side)
        onward(line - 1, side).start()
    multiply(line - 2)
    multiply_short(line - 2)
    short_arrivals(line - 1)
    multiply_short(line - 1)
    multiply(line - 1)

    lanes = lax.broadcasted_iota(jnp.int32, (TILE, LANES), 1)
    per_tile = TILE // own
    for tile in range(tiles):
        part = logits[tile * TILE : (tile + 1) * TILE, :]
        top = jnp.max(part, axis=1, keepdims=True)
        exponent = jnp.exp(part - top)
        upper = exponent.astype(jnp.bfloat16)
        lower = (exponent - upper.astype(jnp.float32)).astype(jnp.bfloat16)
        weighted = jnp.dot(upper, table[...], preferred_element_type=jnp.float32) + jnp.dot(
            lower, table[...], preferred_element_type=jnp.float32
        )
        stat[tile * TILE : (tile + 1) * TILE, :] = jnp.where(lanes == width + 1, top, weighted)
        for device in range(tile * per_tile, (tile + 1) * per_tile):

            @pl.when(me != device)
            def _():
                send(
                    stat.at[pl.ds(device * own, own)],
                    stat_in.at[slot(device)],
                    stat_sems.at[0],
                    stat_sems.at[1],
                    {"vocab": device},
                ).start()

    position = lax.broadcasted_iota(jnp.int32, (TILE, LANES), 0)
    masked_in = []
    for tile in range(tiles):
        valid = (position < lengths_ref[row * tiles + tile]).astype(jnp.float32)
        masked_in.append(inner[tile * TILE : (tile + 1) * TILE, :] * valid[:, :width])
    flat_in = jnp.concatenate(masked_in, axis=0)
    padded_in = jnp.concatenate([jnp.zeros_like(flat_in), flat_in], axis=1)
    mix[row, tiles] = dot_f32(flat_in, padded_in, ((0,), (0,)))

    await_bytes(pick_in, pick_sems.at[1])
    picked = own_part(pick, me)[...].astype(jnp.float32)
    for other in range(count - 1):
        picked = picked + pick_in[other].astype(jnp.float32)
    await_bytes(stat_in, stat_sems.at[1])
    mine = own_part(stat, me)[...]
    tops = [mine[:, width + 1 : width + 2]]
    for other in range(count - 1):
        tops.append(stat_in[other][:, width + 1 : width + 2])
    joint = functools.reduce(jnp.maximum, tops)
    total = mine * jnp.exp(tops[0] - joint)
    for other in range(count - 1):
        total = total + stat_in[other] * jnp.exp(tops[other + 1] - joint)
    first = me * own
    place_in_tile = lax.broadcasted_iota(jnp.int32, (own, LANES), 0) + first % TILE
    valid = (place_in_tile < lengths_ref[row * tiles + first // TILE]).astype(jnp.float32)
    finished = (total / total[:, width : width + 1] - picked) * valid
    grad[...] = jnp.concatenate([finished[: own // 2, :width], finished[own // 2 :, :width]], axis=1)

    def send_grad(step, carry):
        device = (me + step) % count
        send(grad, grad_in.at[me], grad_sems.at[0], grad_sems.at[1], {"vocab": device}).start()
        return carry

    lax.fori_loop(1, count, send_grad, 0)
    grad_in[me] = grad[...]
    await_bytes(grad_in.at[pl.ds(0, count - 1)], grad_sems.at[1])

    for tile in range(tiles):
        pieces = []
        for other in range(tile * per_tile, (tile + 1) * per_tile):
            pieces += [grad_in[other][:, :width], grad_in[other][:, width:]]
        grads = jnp.concatenate(pieces, axis=0)
        joined_sides = jnp.concatenate([grads, masked_in[tile]], axis=1)
        mix[row, tile] = dot_f32(grads, joined_sides, ((0,), (0,)))
    mix_copies = []
    for step in range(1, parts):
        copy = send(
            mix.at[row], mix_in.at[row], mix_send.at[step], mix_recv.at[row], {"rows": (row + step) % parts}
        )
        copy.start()
        mix_copies.append(copy)
    mix_in[row] = mix[row]
    for step in range(1, parts):
        other = (row + step) % parts
        send(mix.at[row], mix_in.at[other], mix_send.at[0], mix_recv.at[other], {"rows": row}).wait_recv()

    row_total = lengths_ref[0]
    for sequence in range(1, seq_count):
        row_total = row_total + lengths_ref[sequence]
    one_over = 1.0 / jnp.full((1, LANES), row_total, jnp.int32).astype(jnp.float32)
    cov_out = jnp.zeros((width, LANES), jnp.float32)
    cov_in = jnp.zeros((width, LANES), jnp.float32)
    for part in range(parts):
        for tile in range(tiles):
            cov_out = cov_out + mix_in[part, tile]
        cov_in = cov_in + mix_in[part, tiles]
    left = lax.broadcasted_iota(jnp.int32, (width, LANES), 1) < width
    cov = jnp.concatenate([jnp.where(left, cov_out, 0.0), cov_in], axis=0) * one_over
    identity = (
        lax.broadcasted_iota(jnp.int32, (LANES, LANES), 0)
        == lax.broadcasted_iota(jnp.int32, (LANES, LANES), 1)
    ).astype(jnp.float32)
    diagonal = jnp.sum(cov * identity, axis=0, keepdims=True)
    left_row = lax.broadcasted_iota(jnp.int32, (1, LANES), 1) < width
    trace_out = jnp.sum(jnp.where(left_row, diagonal, 0.0), axis=1, keepdims=True)
    trace_in = jnp.sum(jnp.where(left_row, 0.0, diagonal), axis=1, keepdims=True)
    trace = jnp.where(left_row, trace_out, trace_in)
    damp = damping_ratio * trace / width + tiny_value
    middle = damp + 0.5 * trace
    scaled = (cov + identity * damp) * (1.0 / middle)
    reach = 1.0 / (1.0 + 2.0 * damping_ratio / width)
    gain = 2.0 / (2.0 - reach * reach)
    inverse = gain * (2.0 * identity - scaled)
    reach = reach * reach / (2.0 - reach * reach)
    while reach > 1e-8:
        gain = 2.0 / (2.0 - reach * reach)
        reach = reach * reach / (2.0 - reach * reach)
        if reach > 1e-3:
            inverse = gain * (2.0 * inverse - dot_three(inverse, dot_three(scaled, inverse)))
        else:
            again = dot_f32(scaled, inverse, ((1,), (0,)))
            inverse = gain * (2.0 * inverse - dot_f32(inverse, again, ((1,), (0,))))
    inverse = inverse * (1.0 / middle)
    stacked = []
    for part in range(parts):
        for tile in range(tiles):
            long = jnp.full((1, LANES), lengths_ref[part * tiles + tile], jnp.int32)
            stacked.append(mix_in[part, tile] * lax.rsqrt(long.astype(jnp.float32)))
    right = dot_three(jnp.concatenate(stacked, axis=0), inverse)
    corner = inverse[:width, :width]
    for sequence in range(seq_count):
        rows = slice(sequence * width, (sequence + 1) * width)
        white[rows, :] = dot_three(corner, right[rows, :])
    for pair in range(width // 2):
        even = white[pl.ds(2 * pair, seq_count, stride=width), :]
        odd = white[pl.ds(2 * pair + 1, seq_count, stride=width), :]
        flat[:, pair * LANES : (pair + 1) * LANES] = jnp.concatenate(
            [even[:, width:], odd[:, width:]], axis=1
        )
    local_store.wait()
    scores_ref[...] = lax.dot_general(
        flat[...].astype(jnp.bfloat16),
        store[...],
        (((1,), (1,)), ((), ())),
        preferred_element_type=jnp.float32,
    )

    for k in range(line):
        for side in range(2):
            outward(k, side, lambda copy: copy.wait_send())
            onward(k, side).wait_send()
        for side in (2, 3):
            for pair in range(4):
                if k > 0:
                    along(k, side, pair, lambda copy: copy.wait_send())
                elif pair > 0:
                    short_onward(pair, side, lambda copy: copy.wait_send())
                else:
                    short_start(side, lambda copy: copy.wait_send())
    for copy in head_copies + mix_copies:
        copy.wait_send()
    await_bytes(pick_in, pick_sems.at[0])
    await_bytes(stat_in, stat_sems.at[0])
    await_bytes(grad_in.at[pl.ds(0, count - 1)], grad_sems.at[0])


def class_rows(tokens):
    short = tokens // 10 // 16 * 16
    return tokens // 2 - short, short


def per_device_any(count, parts, hidden, head_weight, in_proj, out_proj, targets, lengths, grad_store):
    tokens, block = hidden.shape
    vocab_cols = head_weight.shape[1]
    width = in_proj.shape[1]
    own = tokens // count
    tiles = tokens // TILE
    fits = (
        count % 4 == 0
        and block % LANES == 0
        and 2 * width == LANES
        and own % 32 == 0
        and tokens % 32 == 0
        and tokens >= 160
        and TILE % own == 0
        and grad_store.shape[1] == width * width
    )
    if not fits:
        return per_device(hidden, head_weight, in_proj, out_proj, targets, lengths, grad_store)
    line = count // 4
    seq_count = lengths.shape[0]
    hbm = pl.BlockSpec(memory_space=pltpu.HBM)
    vmem = pl.BlockSpec(memory_space=pltpu.VMEM)
    dma = pltpu.SemaphoreType.DMA
    f32, bf16 = jnp.float32, jnp.bfloat16
    return pl.pallas_call(
        functools.partial(kernel, line, parts),
        out_shape=jax.ShapeDtypeStruct((seq_count, grad_store.shape[0]), f32),
        in_specs=[hbm] * 7,
        out_specs=vmem,
        scratch_shapes=[
            pltpu.VMEM((count, tokens, block), bf16),
            pltpu.VMEM((head_weight.shape[0] * parts, vocab_cols), bf16),
            pltpu.VMEM((tokens, vocab_cols), f32),
            pltpu.VMEM((tokens, width), f32),
            pltpu.VMEM(grad_store.shape, bf16),
            pltpu.VMEM(in_proj.shape[::-1], bf16),
            pltpu.VMEM(out_proj.shape[::-1], bf16),
            pltpu.VMEM((1, tokens), jnp.int32),
            pltpu.SMEM(lengths.shape, jnp.int32),
            pltpu.VMEM((vocab_cols, LANES), bf16),
            pltpu.VMEM((tokens, LANES), bf16),
            pltpu.VMEM((count - 1, own, LANES), bf16),
            pltpu.VMEM((tokens, LANES), f32),
            pltpu.VMEM((count - 1, own, LANES), f32),
            pltpu.VMEM((own // 2, LANES), f32),
            pltpu.VMEM((count, own // 2, LANES), f32),
            pltpu.VMEM((parts, tiles + 1, width, LANES), f32),
            pltpu.VMEM((parts, tiles + 1, width, LANES), f32),
            pltpu.VMEM((seq_count * width, LANES), f32),
            pltpu.VMEM((seq_count, width * width), f32),
            dma((7,)),
            dma((parts,)),
            dma((parts,)),
            dma((4, 4, count)),
            dma((4, count)),
            dma((2,)),
            dma((2,)),
            dma((2,)),
            dma((parts,)),
            dma((parts,)),
        ],
        compiler_params=pltpu.CompilerParams(
            collective_id=0, has_side_effects=True, vmem_limit_bytes=64 * 1024 * 1024
        ),
        cost_estimate=pl.CostEstimate(
            flops=2 * tokens * block * count * vocab_cols,
            bytes_accessed=4 * tokens * block * count,
            transcendentals=tokens * vocab_cols,
        ),
    )(hidden, head_weight, in_proj.T, out_proj.T, targets[None, :], lengths, grad_store)


def solution(mesh):
    return jax.shard_map(
        functools.partial(per_device_any, mesh.shape["vocab"], mesh.shape["rows"]),
        mesh=mesh,
        in_specs=(
            P("rows", "vocab"),
            P("rows", "vocab"),
            P(),
            P("vocab", None),
            P("rows"),
            P(),
            P(("vocab", "rows"), None),
        ),
        out_specs=P(None, ("vocab", "rows")),
        check_vma=False,
    )
```

```python
import functools

import jax
import jax.numpy as jnp
from jax import lax
from jax.experimental import pallas as pl
from jax.experimental.pallas import tpu as pltpu
from jax.sharding import PartitionSpec as P

TILE = 128


damping_ratio = 0.1
tiny_value = 1e-06


def joined(value, axis, join):
    pieces = jax.tree.map(lambda part: lax.all_gather(part, axis), value)
    head = jax.tree.map(lambda part: part[0], pieces)
    tail = jax.tree.map(lambda part: part[1:], pieces)
    running, _ = lax.scan(lambda running, slab: (join(running, slab), None), head, tail)
    return running


def whiten(seq_grads, cov_out, cov_in):
    proj_width = cov_out.shape[0]
    seq_count = seq_grads.shape[0]
    identity = jnp.eye(proj_width, dtype=jnp.float32)
    damp_out = damping_ratio * jnp.trace(cov_out) / proj_width + tiny_value
    damp_in = damping_ratio * jnp.trace(cov_in) / proj_width + tiny_value
    lower_out = jnp.linalg.cholesky(cov_out + damp_out * identity)
    lower_in = jnp.linalg.cholesky(cov_in + damp_in * identity)
    stacked = jnp.transpose(seq_grads, (1, 0, 2)).reshape(proj_width, seq_count * proj_width)
    left_half = lax.linalg.triangular_solve(lower_out, stacked, left_side=True, lower=True)
    left_full = lax.linalg.triangular_solve(
        lower_out, left_half, left_side=True, lower=True, transpose_a=True
    )
    rows_form = jnp.transpose(
        left_full.reshape(proj_width, seq_count, proj_width), (1, 0, 2)
    ).reshape(seq_count * proj_width, proj_width)
    right_half = lax.linalg.triangular_solve(
        lower_in, rows_form, left_side=False, lower=True, transpose_a=True
    )
    right_full = lax.linalg.triangular_solve(lower_in, right_half, left_side=False, lower=True)
    return right_full.reshape(seq_count, proj_width * proj_width)


def combine_rows(earlier, later):
    max_one, sum_one, weight_one = earlier
    max_two, sum_two, weight_two = later
    joint_max = jnp.maximum(max_one, max_two)
    scale_one = jnp.exp(max_one - joint_max)
    scale_two = jnp.exp(max_two - joint_max)
    joint_sum = sum_one * scale_one + sum_two * scale_two
    joint_weight = weight_one * scale_one[:, None] + weight_two * scale_two[:, None]
    return (joint_max, joint_sum, joint_weight)


def per_device(hidden, head_weight, in_proj, out_proj, targets, lengths, grad_store):
    token_count = hidden.shape[0]
    vocab_cols = head_weight.shape[1]
    proj_width = in_proj.shape[1]
    tile_count = token_count // TILE
    features = lax.all_gather(hidden, "vocab", axis=1, tiled=True)
    out_table = out_proj.astype(jnp.float32)
    first_column = lax.axis_index("vocab") * vocab_cols
    column_ids = lax.broadcasted_iota(jnp.int32, (token_count, vocab_cols), 1) + first_column
    onehot = (column_ids == targets[:, None]).astype(jnp.float32)
    picked_local = jnp.dot(onehot, out_table, precision=lax.Precision.HIGHEST)
    picked = lax.psum(picked_local, "vocab")
    logits = jnp.dot(
        features,
        lax.all_gather(head_weight, "rows", axis=0, tiled=True),
        preferred_element_type=jnp.float32,
    )
    local_max = jnp.max(logits, axis=1)
    exponent = jnp.exp(logits - local_max[:, None])
    weighted = jnp.dot(exponent, out_table, precision=lax.Precision.HIGHEST)
    merged = joined((local_max, jnp.sum(exponent, axis=1), weighted), "vocab", combine_rows)
    out_grad = merged[2] / merged[1][:, None] - picked
    input_proj = jnp.dot(features, in_proj, preferred_element_type=jnp.float32)
    own_lengths = lax.dynamic_slice_in_dim(lengths, lax.axis_index("rows") * tile_count, tile_count)
    position = lax.broadcasted_iota(jnp.int32, (tile_count, TILE), 1)
    is_valid = (position < own_lengths[:, None]).astype(jnp.float32)[:, :, None]
    out_tiles = out_grad.reshape(tile_count, TILE, proj_width) * is_valid
    in_tiles = input_proj.reshape(tile_count, TILE, proj_width) * is_valid
    flat_out = out_tiles.reshape(token_count, proj_width)
    flat_in = in_tiles.reshape(token_count, proj_width)
    local_out = jnp.dot(flat_out.T, flat_out, precision=lax.Precision.HIGHEST)
    local_in = jnp.dot(flat_in.T, flat_in, precision=lax.Precision.HIGHEST)
    cov_out, cov_in = lax.psum((local_out, local_in), "rows")
    row_total = jnp.sum(lengths).astype(jnp.float32)
    seq_grads = jnp.einsum("stk,stj->skj", out_tiles, in_tiles, precision=lax.Precision.HIGHEST)
    seq_grads = seq_grads / jnp.sqrt(own_lengths.astype(jnp.float32))[:, None, None]
    whitened = whiten(seq_grads, cov_out / row_total, cov_in / row_total).astype(jnp.bfloat16)
    return jnp.dot(
        lax.all_gather(whitened, "rows", axis=0, tiled=True),
        grad_store.T,
        preferred_element_type=jnp.float32,
    )


LANES = 128
HIGHEST = lax.Precision.HIGHEST
MESH = pl.DeviceIdType.MESH


def dot_f32(left, right, dims):
    return lax.dot_general(
        left, right, (dims, ((), ())), precision=HIGHEST, preferred_element_type=jnp.float32
    )


def split(value):
    upper = value.astype(jnp.bfloat16)
    return upper, (value - upper.astype(jnp.float32)).astype(jnp.bfloat16)


def dot_three(left, right):
    left_upper, left_lower = split(left)
    right_upper, right_lower = split(right)
    small = jnp.dot(left_upper, right_lower, preferred_element_type=jnp.float32) + jnp.dot(
        left_lower, right_upper, preferred_element_type=jnp.float32
    )
    return small + jnp.dot(left_upper, right_upper, preferred_element_type=jnp.float32)


def damped_inverse(cov):
    width = cov.shape[0]
    identity = (
        lax.broadcasted_iota(jnp.int32, cov.shape, 0) == lax.broadcasted_iota(jnp.int32, cov.shape, 1)
    ).astype(jnp.float32)
    diagonal = jnp.sum(cov * identity, axis=0, keepdims=True)
    trace = jnp.sum(diagonal, axis=1, keepdims=True)
    damp = damping_ratio * trace / width + tiny_value
    shrink = 1.0 / (damp + 0.5 * trace)
    scaled = (cov + identity * damp) * shrink
    reach = 1.0 / (1.0 + 2.0 * damping_ratio / width)
    gain = 2.0 / (2.0 - reach * reach)
    inverse = gain * (2.0 * identity - scaled)
    reach = reach * reach / (2.0 - reach * reach)
    while reach > 1e-8:
        gain = 2.0 / (2.0 - reach * reach)
        reach = reach * reach / (2.0 - reach * reach)
        if reach > 1e-3:
            inverse = gain * (2.0 * inverse - dot_three(inverse, dot_three(scaled, inverse)))
        else:
            again = dot_f32(scaled, inverse, ((1,), (0,)))
            inverse = gain * (2.0 * inverse - dot_f32(inverse, again, ((1,), (0,))))
    return inverse * shrink


def kernel(
    line,
    parts,
    hidden_ref,
    head_ref,
    in_proj_hbm,
    out_proj_hbm,
    targets_hbm,
    lengths_hbm,
    store_ref,
    scores_ref,
    feat,
    weights,
    logits,
    inner,
    store,
    in_proj_ref,
    out_proj_ref,
    targets_ref,
    lengths_ref,
    table,
    pick,
    pick_in,
    stat,
    stat_in,
    grad,
    grad_in,
    side_in,
    mix,
    mix_in,
    white,
    flat,
    load_sem,
    head_send,
    head_recv,
    feat_send,
    feat_recv,
    pick_sems,
    stat_sems,
    grad_sems,
    side_send,
    side_recv,
    mix_send,
    mix_recv,
):
    count = line * 4
    me = lax.axis_index("vocab")
    row = lax.axis_index("rows")
    z, y, x = me // 4, (me // 2) % 2, me % 2
    tokens, block = hidden_ref.shape
    long_rows, short_rows = class_rows(tokens)
    starts = (0, long_rows, 2 * long_rows, 2 * long_rows + short_rows)
    sizes = (long_rows, long_rows, short_rows, short_rows)
    depth, vocab_cols = head_ref.shape
    width = out_proj_ref.shape[0]
    own = tokens // count
    tiles = tokens // TILE
    seq_count = tiles * parts

    def send(source, target, send_sem, recv_sem, device):
        return pltpu.make_async_remote_copy(
            src_ref=source,
            dst_ref=target,
            send_sem=send_sem,
            recv_sem=recv_sem,
            device_id=device,
            device_id_type=MESH,
        )

    def await_bytes(ref, sem):
        pltpu.make_async_copy(ref, ref, sem).wait()

    barrier = pltpu.get_barrier_semaphore()

    def greet(step, carry):
        pl.semaphore_signal(
            barrier, inc=1, device_id={"vocab": (me + step) % count}, device_id_type=MESH
        )
        return carry

    lax.fori_loop(1, count, greet, 0)
    for step in range(1, parts):
        pl.semaphore_signal(
            barrier, inc=1, device_id={"rows": (row + step) % parts}, device_id_type=MESH
        )
    local_feat = pltpu.make_async_copy(hidden_ref, feat.at[me], load_sem.at[0])
    local_store = pltpu.make_async_copy(store_ref, store, load_sem.at[2])
    local_feat.start()
    small = [
        pltpu.make_async_copy(source, target, load_sem.at[3 + at])
        for at, (source, target) in enumerate(
            [
                (out_proj_hbm, out_proj_ref),
                (targets_hbm, targets_ref),
                (lengths_hbm, lengths_ref),
                (in_proj_hbm, in_proj_ref),
            ]
        )
    ]
    for copy in small:
        copy.start()
    chunk = 4 * block
    per_part = line // parts

    def head_chunk(zz):
        return weights.at[pl.ds(pl.multiple_of(zz * chunk, chunk), chunk)]

    for at in range(per_part):
        pltpu.make_async_copy(
            head_ref.at[pl.ds(at * chunk, chunk)],
            head_chunk(row * per_part + at),
            head_recv.at[row * per_part + at],
        ).start()
    local_store.start()
    pl.semaphore_wait(barrier, count - 1 + parts - 1)

    def place(zz, yy, xx):
        return (zz * 2 + yy) * 2 + xx

    def item(zz, side, pair):
        near, far = pair % 2, pair // 2
        flip_y, flip_x = (far, near) if side % 2 == 0 else (near, far)
        return place(zz, (y + flip_y) % 2, (x + flip_x) % 2)

    def piece(index, side):
        return feat.at[index, pl.ds(starts[side], sizes[side])]

    def hop(index, side, route, device, source=None):
        return send(
            piece(index, side) if source is None else source,
            piece(index, side),
            feat_send.at[route, side, index],
            feat_recv.at[side, index],
            {"vocab": device},
        )

    nearest = jnp.minimum(z, line - 1 - z)

    def nth(k):
        if k == 0:
            return z
        sign_near = -1 if k % 2 == 1 else 1
        sign_far = jnp.where(z < line - 1 - z, 1, -1)
        return z + jnp.where(k <= 2 * nearest, sign_near * ((k + 1) // 2), sign_far * (k - nearest))

    def own_rows_of(side):
        return hidden_ref.at[pl.ds(starts[side], sizes[side])]

    def along(k, side, pair, action, source=None):
        zz = nth(k)
        index = item(zz, side, pair)
        up = z < line - 1
        down = z > 0
        if k > 0:
            up = jnp.logical_and(zz < z, up)
            down = jnp.logical_and(zz > z, down)

        @pl.when(up)
        def _():
            action(hop(index, side, 0, place(jnp.minimum(z + 1, line - 1), y, x), source))

        @pl.when(down)
        def _():
            action(hop(index, side, 1, place(jnp.maximum(z - 1, 0), y, x), source))

    def outward(k, side, action):
        source = own_rows_of(side) if k == 0 else None
        index = item(nth(k), side, 0)
        along(k, side, 0, action, source)
        action(hop(index, side, 2, item(z, side, 1), source))
        action(hop(index, side, 3, item(z, side, 2), source))

    def onward(k, side):
        return hop(item(nth(k), side, 1), side, 2, item(z, side, 2))

    def arrived(index, side):
        hop(index, side, 0, me).wait_recv()

    def accumulate(index, start, size):
        rows = pl.ds(pl.multiple_of(start, 16), size)
        columns = pl.ds(pl.multiple_of(index * block, block), block)
        features = feat[index, rows, :]
        logits[rows, :] += jnp.dot(
            features, weights[columns, :], preferred_element_type=jnp.float32
        )
        inner[rows, :] += lax.dot_general(
            features,
            in_proj_ref[:, columns],
            (((1,), (1,)), ((), ())),
            preferred_element_type=jnp.float32,
        )

    def multiply(k):
        zz = nth(k)
        pltpu.make_async_copy(head_chunk(zz), head_chunk(zz), head_recv.at[zz]).wait()

        def body(step, carry):
            side, pair = step % 2, step // 2
            near, far = pair % 2, pair // 2
            flip_x = (1 - side) * near + side * far
            flip_y = (1 - side) * far + side * near
            index = place(zz, (y + flip_y) % 2, (x + flip_x) % 2)

            @pl.when(pair >= 2)
            def _():
                pltpu.make_async_copy(
                    piece(index, 0), piece(index, 0), feat_recv.at[side, index]
                ).wait()

            accumulate(index, side * long_rows, long_rows)
            return carry

        lax.fori_loop(0, 8, body, 0)

    def multiply_short(k):
        zz = nth(k)

        def body(pair, carry):
            index = place(zz, (y + pair // 2) % 2, (x + pair % 2) % 2)
            accumulate(index, 2 * long_rows, 2 * short_rows)
            return carry

        lax.fori_loop(0, 4, body, 0)

    def short_arrivals(k):
        for pair in range(4):
            for side in (2, 3):
                if k > 0:
                    arrived(item(nth(k), side, pair), side)
                    along(k, side, pair, lambda copy: copy.start())

    def short_start(side, action):
        source = own_rows_of(side)
        action(hop(me, side, 2, item(z, side, 1), source))
        action(hop(me, side, 3, item(z, side, 2), source))
        along(0, side, 0, action, source)

    def short_onward(pair, side, action):
        index = item(z, side, pair)
        if pair == 1:
            action(hop(index, side, 2, item(z, side, 2)))
        along(0, side, pair, action)

    for side in (2, 3):
        short_start(side, lambda copy: copy.start())
    for side in range(2):
        outward(0, side, lambda copy: copy.start())
    def head_copy(k, step):
        zz = nth(k)
        at = zz % per_part
        return send(
            head_ref.at[pl.ds(pl.multiple_of(at * chunk, chunk), chunk)],
            head_chunk(zz),
            head_send.at[step, zz],
            head_recv.at[zz],
            {"rows": (row + step) % parts},
        )

    def head_sends(action):
        for k in range(line):

            @pl.when(nth(k) // per_part == row)
            def _():
                for step in range(1, parts):
                    action(head_copy(k, step))

    head_sends(lambda copy: copy.start())

    for copy in small:
        copy.wait()
    marker = lax.broadcasted_iota(jnp.int32, (LANES - width, vocab_cols), 0)
    upright = jnp.concatenate([out_proj_ref[...].astype(jnp.float32), (marker == 0).astype(jnp.float32)], axis=0)
    table[...] = upright.T.astype(jnp.bfloat16)
    column_ids = lax.broadcasted_iota(jnp.int32, (vocab_cols, tokens), 0) + me * vocab_cols
    onehot = (column_ids == targets_ref[...]).astype(jnp.float32).astype(jnp.bfloat16)
    pick[...] = jnp.dot(
        upright.astype(jnp.bfloat16), onehot, preferred_element_type=jnp.float32
    ).T.astype(jnp.bfloat16)

    def own_part(ref, device):
        return ref.at[pl.ds(pl.multiple_of(device * own, own), own)]

    def slot(device):
        return (me - device - 1 + 2 * count) % count

    def send_pick(step, carry):
        device = (me + step) % count
        send(
            own_part(pick, device),
            pick_in.at[slot(device)],
            pick_sems.at[0],
            pick_sems.at[1],
            {"vocab": device},
        ).start()
        return carry

    lax.fori_loop(1, count, send_pick, 0)
    logits[...] = jnp.zeros_like(logits)
    inner[...] = jnp.zeros_like(inner)

    for k in range(line):
        if k == 1:
            for pair in (1, 2, 3):
                for side in (2, 3):
                    arrived(item(z, side, pair), side)
                    short_onward(pair, side, lambda copy: copy.start())
        if k > 0:
            for side in range(2):
                arrived(place(nth(k), y, x), side)
                outward(k, side, lambda copy: copy.start())
            for side in range(2):
                arrived(item(nth(k - 1), side, 1), side)
                onward(k - 1, side).start()
            short_arrivals(k - 1)
        if k == 1:
            local_feat.wait()
        if k > 1:
            multiply(k - 2)
            multiply_short(k - 2)
    for side in range(2):
        arrived(item(nth(line - 1), side, 1), side)
        onward(line - 1, side).start()
    multiply(line - 2)
    multiply_short(line - 2)
    short_arrivals(line - 1)
    multiply(line - 1)
    multiply_short(line - 1)

    lanes = lax.broadcasted_iota(jnp.int32, (TILE, LANES), 1)
    per_tile = TILE // own
    for tile in range(tiles):
        part = logits[tile * TILE : (tile + 1) * TILE, :]
        top = jnp.max(part, axis=1, keepdims=True)
        exponent = jnp.exp(part - top)
        upper = exponent.astype(jnp.bfloat16)
        lower = (exponent - upper.astype(jnp.float32)).astype(jnp.bfloat16)
        weighted = jnp.dot(upper, table[...], preferred_element_type=jnp.float32) + jnp.dot(
            lower, table[...], preferred_element_type=jnp.float32
        )
        stat[tile * TILE : (tile + 1) * TILE, :] = jnp.where(lanes == width + 1, top, weighted)
        for device in range(tile * per_tile, (tile + 1) * per_tile):

            @pl.when(me != device)
            def _():
                send(
                    stat.at[pl.ds(device * own, own)],
                    stat_in.at[slot(device)],
                    stat_sems.at[0],
                    stat_sems.at[1],
                    {"vocab": device},
                ).start()

    position = lax.broadcasted_iota(jnp.int32, (TILE, LANES), 0)
    masked_in = []
    for tile in range(tiles):
        valid = (position < lengths_ref[row * tiles + tile]).astype(jnp.float32)
        masked_in.append(inner[tile * TILE : (tile + 1) * TILE, :] * valid[:, :width])
    flat_in = jnp.concatenate(masked_in, axis=0)
    side_in[row] = dot_f32(flat_in, flat_in, ((0,), (0,)))
    side_copies = []
    for step in range(1, parts):
        copy = send(
            side_in.at[row], side_in.at[row], side_send.at[step], side_recv.at[row], {"rows": (row + step) % parts}
        )
        copy.start()
        side_copies.append(copy)
    row_total = lengths_ref[0]
    for sequence in range(1, seq_count):
        row_total = row_total + lengths_ref[sequence]
    one_over = 1.0 / jnp.full((1, width), row_total, jnp.int32).astype(jnp.float32)
    for k in range(line):
        for side in range(2):
            outward(k, side, lambda copy: copy.wait_send())
            onward(k, side).wait_send()
        for side in (2, 3):
            for pair in range(4):
                if k > 0:
                    along(k, side, pair, lambda copy: copy.wait_send())
                elif pair > 0:
                    short_onward(pair, side, lambda copy: copy.wait_send())
                else:
                    short_start(side, lambda copy: copy.wait_send())
    head_sends(lambda copy: copy.wait_send())
    for step in range(1, parts):
        other = (row + step) % parts
        send(side_in.at[row], side_in.at[other], side_send.at[0], side_recv.at[other], {"rows": row}).wait_recv()
    cov_in = side_in[0]
    for part in range(1, parts):
        cov_in = cov_in + side_in[part]
    inverse_in = damped_inverse(cov_in * one_over)
    flat_in = dot_three(flat_in, inverse_in)

    await_bytes(pick_in, pick_sems.at[1])
    picked = own_part(pick, me)[...].astype(jnp.float32)
    for other in range(count - 1):
        picked = picked + pick_in[other].astype(jnp.float32)
    await_bytes(stat_in, stat_sems.at[1])
    mine = own_part(stat, me)[...]
    tops = [mine[:, width + 1 : width + 2]]
    for other in range(count - 1):
        tops.append(stat_in[other][:, width + 1 : width + 2])
    joint = functools.reduce(jnp.maximum, tops)
    total = mine * jnp.exp(tops[0] - joint)
    for other in range(count - 1):
        total = total + stat_in[other] * jnp.exp(tops[other + 1] - joint)
    first = me * own
    place_in_tile = lax.broadcasted_iota(jnp.int32, (own, LANES), 0) + first % TILE
    valid = (place_in_tile < lengths_ref[row * tiles + first // TILE]).astype(jnp.float32)
    finished = (total / total[:, width : width + 1] - picked) * valid
    grad[...] = jnp.concatenate([finished[: own // 2, :width], finished[own // 2 :, :width]], axis=1)

    def send_grad(step, carry):
        device = (me + step) % count
        send(grad, grad_in.at[me], grad_sems.at[0], grad_sems.at[1], {"vocab": device}).start()
        return carry

    lax.fori_loop(1, count, send_grad, 0)
    grad_in[me] = grad[...]
    await_bytes(grad_in.at[pl.ds(0, count - 1)], grad_sems.at[1])

    for tile in range(tiles):
        pieces = []
        for other in range(tile * per_tile, (tile + 1) * per_tile):
            pieces += [grad_in[other][:, :width], grad_in[other][:, width:]]
        grads = jnp.concatenate(pieces, axis=0)
        joined_sides = jnp.concatenate([grads, flat_in[tile * TILE : (tile + 1) * TILE, :]], axis=1)
        mix[row, tile] = dot_f32(grads, joined_sides, ((0,), (0,)))
    mix_copies = []
    for step in range(1, parts):
        copy = send(
            mix.at[row], mix_in.at[row], mix_send.at[step], mix_recv.at[row], {"rows": (row + step) % parts}
        )
        copy.start()
        mix_copies.append(copy)
    mix_in[row] = mix[row]
    for step in range(1, parts):
        other = (row + step) % parts
        send(mix.at[row], mix_in.at[other], mix_send.at[0], mix_recv.at[other], {"rows": row}).wait_recv()

    cov_out = jnp.zeros((width, LANES), jnp.float32)
    stacked = []
    for part in range(parts):
        for tile in range(tiles):
            block_mix = mix_in[part, tile]
            cov_out = cov_out + block_mix
            long = jnp.full((1, LANES), lengths_ref[part * tiles + tile], jnp.int32)
            stacked.append(block_mix * lax.rsqrt(long.astype(jnp.float32)))
    inverse_out = damped_inverse(cov_out[:, :width] * one_over)
    whitened = dot_three(inverse_out, jnp.concatenate(stacked, axis=1))
    for sequence in range(seq_count):
        white[sequence * width : (sequence + 1) * width, :] = whitened[
            :, sequence * LANES : (sequence + 1) * LANES
        ]
    for pair in range(width // 2):
        even = white[pl.ds(2 * pair, seq_count, stride=width), :]
        odd = white[pl.ds(2 * pair + 1, seq_count, stride=width), :]
        flat[:, pair * LANES : (pair + 1) * LANES] = jnp.concatenate(
            [even[:, width:], odd[:, width:]], axis=1
        )
    local_store.wait()
    scores_ref[...] = lax.dot_general(
        flat[...].astype(jnp.bfloat16),
        store[...],
        (((1,), (1,)), ((), ())),
        preferred_element_type=jnp.float32,
    )

    for copy in side_copies + mix_copies:
        copy.wait_send()
    await_bytes(pick_in, pick_sems.at[0])
    await_bytes(stat_in, stat_sems.at[0])
    await_bytes(grad_in.at[pl.ds(0, count - 1)], grad_sems.at[0])


def class_rows(tokens):
    short = tokens // 10 // 16 * 16
    return tokens // 2 - short, short


def per_device_any(count, parts, hidden, head_weight, in_proj, out_proj, targets, lengths, grad_store):
    tokens, block = hidden.shape
    vocab_cols = head_weight.shape[1]
    width = in_proj.shape[1]
    own = tokens // count
    tiles = tokens // TILE
    fits = (
        count % (4 * parts) == 0
        and block % LANES == 0
        and 2 * width == LANES
        and own % 32 == 0
        and tokens % 32 == 0
        and tokens >= 160
        and TILE % own == 0
        and grad_store.shape[1] == width * width
    )
    if not fits:
        return per_device(hidden, head_weight, in_proj, out_proj, targets, lengths, grad_store)
    line = count // 4
    seq_count = lengths.shape[0]
    hbm = pl.BlockSpec(memory_space=pltpu.HBM)
    vmem = pl.BlockSpec(memory_space=pltpu.VMEM)
    dma = pltpu.SemaphoreType.DMA
    f32, bf16 = jnp.float32, jnp.bfloat16
    return pl.pallas_call(
        functools.partial(kernel, line, parts),
        out_shape=jax.ShapeDtypeStruct((seq_count, grad_store.shape[0]), f32),
        in_specs=[hbm] * 7,
        out_specs=vmem,
        scratch_shapes=[
            pltpu.VMEM((count, tokens, block), bf16),
            pltpu.VMEM((head_weight.shape[0] * parts, vocab_cols), bf16),
            pltpu.VMEM((tokens, vocab_cols), f32),
            pltpu.VMEM((tokens, width), f32),
            pltpu.VMEM(grad_store.shape, bf16),
            pltpu.VMEM(in_proj.shape[::-1], bf16),
            pltpu.VMEM(out_proj.shape[::-1], bf16),
            pltpu.VMEM((1, tokens), jnp.int32),
            pltpu.SMEM(lengths.shape, jnp.int32),
            pltpu.VMEM((vocab_cols, LANES), bf16),
            pltpu.VMEM((tokens, LANES), bf16),
            pltpu.VMEM((count - 1, own, LANES), bf16),
            pltpu.VMEM((tokens, LANES), f32),
            pltpu.VMEM((count - 1, own, LANES), f32),
            pltpu.VMEM((own // 2, LANES), f32),
            pltpu.VMEM((count, own // 2, LANES), f32),
            pltpu.VMEM((parts, width, width), f32),
            pltpu.VMEM((parts, tiles, width, LANES), f32),
            pltpu.VMEM((parts, tiles, width, LANES), f32),
            pltpu.VMEM((seq_count * width, LANES), f32),
            pltpu.VMEM((seq_count, width * width), f32),
            dma((7,)),
            dma((parts, line)),
            dma((line,)),
            dma((4, 4, count)),
            dma((4, count)),
            dma((2,)),
            dma((2,)),
            dma((2,)),
            dma((parts,)),
            dma((parts,)),
            dma((parts,)),
            dma((parts,)),
        ],
        compiler_params=pltpu.CompilerParams(
            collective_id=0, has_side_effects=True, vmem_limit_bytes=64 * 1024 * 1024
        ),
        cost_estimate=pl.CostEstimate(
            flops=2 * tokens * block * count * vocab_cols,
            bytes_accessed=4 * tokens * block * count,
            transcendentals=tokens * vocab_cols,
        ),
    )(hidden, head_weight, in_proj.T, out_proj.T, targets[None, :], lengths, grad_store)


def solution(mesh):
    return jax.shard_map(
        functools.partial(per_device_any, mesh.shape["vocab"], mesh.shape["rows"]),
        mesh=mesh,
        in_specs=(
            P("rows", "vocab"),
            P("rows", "vocab"),
            P(),
            P("vocab", None),
            P("rows"),
            P(),
            P(("vocab", "rows"), None),
        ),
        out_specs=P(None, ("vocab", "rows")),
        check_vma=False,
    )
```

```python
import functools

import jax
import jax.numpy as jnp
from jax import lax
from jax.experimental import pallas as pl
from jax.experimental.pallas import tpu as pltpu
from jax.sharding import PartitionSpec as P

TILE = 128


damping_ratio = 0.1
tiny_value = 1e-06


def joined(value, axis, join):
    pieces = jax.tree.map(lambda part: lax.all_gather(part, axis), value)
    head = jax.tree.map(lambda part: part[0], pieces)
    tail = jax.tree.map(lambda part: part[1:], pieces)
    running, _ = lax.scan(lambda running, slab: (join(running, slab), None), head, tail)
    return running


def whiten(seq_grads, cov_out, cov_in):
    proj_width = cov_out.shape[0]
    seq_count = seq_grads.shape[0]
    identity = jnp.eye(proj_width, dtype=jnp.float32)
    damp_out = damping_ratio * jnp.trace(cov_out) / proj_width + tiny_value
    damp_in = damping_ratio * jnp.trace(cov_in) / proj_width + tiny_value
    lower_out = jnp.linalg.cholesky(cov_out + damp_out * identity)
    lower_in = jnp.linalg.cholesky(cov_in + damp_in * identity)
    stacked = jnp.transpose(seq_grads, (1, 0, 2)).reshape(proj_width, seq_count * proj_width)
    left_half = lax.linalg.triangular_solve(lower_out, stacked, left_side=True, lower=True)
    left_full = lax.linalg.triangular_solve(
        lower_out, left_half, left_side=True, lower=True, transpose_a=True
    )
    rows_form = jnp.transpose(
        left_full.reshape(proj_width, seq_count, proj_width), (1, 0, 2)
    ).reshape(seq_count * proj_width, proj_width)
    right_half = lax.linalg.triangular_solve(
        lower_in, rows_form, left_side=False, lower=True, transpose_a=True
    )
    right_full = lax.linalg.triangular_solve(lower_in, right_half, left_side=False, lower=True)
    return right_full.reshape(seq_count, proj_width * proj_width)


def combine_rows(earlier, later):
    max_one, sum_one, weight_one = earlier
    max_two, sum_two, weight_two = later
    joint_max = jnp.maximum(max_one, max_two)
    scale_one = jnp.exp(max_one - joint_max)
    scale_two = jnp.exp(max_two - joint_max)
    joint_sum = sum_one * scale_one + sum_two * scale_two
    joint_weight = weight_one * scale_one[:, None] + weight_two * scale_two[:, None]
    return (joint_max, joint_sum, joint_weight)


def per_device(hidden, head_weight, in_proj, out_proj, targets, lengths, grad_store):
    token_count = hidden.shape[0]
    vocab_cols = head_weight.shape[1]
    proj_width = in_proj.shape[1]
    tile_count = token_count // TILE
    features = lax.all_gather(hidden, "vocab", axis=1, tiled=True)
    out_table = out_proj.astype(jnp.float32)
    first_column = lax.axis_index("vocab") * vocab_cols
    column_ids = lax.broadcasted_iota(jnp.int32, (token_count, vocab_cols), 1) + first_column
    onehot = (column_ids == targets[:, None]).astype(jnp.float32)
    picked_local = jnp.dot(onehot, out_table, precision=lax.Precision.HIGHEST)
    picked = lax.psum(picked_local, "vocab")
    logits = jnp.dot(
        features,
        lax.all_gather(head_weight, "rows", axis=0, tiled=True),
        preferred_element_type=jnp.float32,
    )
    local_max = jnp.max(logits, axis=1)
    exponent = jnp.exp(logits - local_max[:, None])
    weighted = jnp.dot(exponent, out_table, precision=lax.Precision.HIGHEST)
    merged = joined((local_max, jnp.sum(exponent, axis=1), weighted), "vocab", combine_rows)
    out_grad = merged[2] / merged[1][:, None] - picked
    input_proj = jnp.dot(features, in_proj, preferred_element_type=jnp.float32)
    own_lengths = lax.dynamic_slice_in_dim(lengths, lax.axis_index("rows") * tile_count, tile_count)
    position = lax.broadcasted_iota(jnp.int32, (tile_count, TILE), 1)
    is_valid = (position < own_lengths[:, None]).astype(jnp.float32)[:, :, None]
    out_tiles = out_grad.reshape(tile_count, TILE, proj_width) * is_valid
    in_tiles = input_proj.reshape(tile_count, TILE, proj_width) * is_valid
    flat_out = out_tiles.reshape(token_count, proj_width)
    flat_in = in_tiles.reshape(token_count, proj_width)
    local_out = jnp.dot(flat_out.T, flat_out, precision=lax.Precision.HIGHEST)
    local_in = jnp.dot(flat_in.T, flat_in, precision=lax.Precision.HIGHEST)
    cov_out, cov_in = lax.psum((local_out, local_in), "rows")
    row_total = jnp.sum(lengths).astype(jnp.float32)
    seq_grads = jnp.einsum("stk,stj->skj", out_tiles, in_tiles, precision=lax.Precision.HIGHEST)
    seq_grads = seq_grads / jnp.sqrt(own_lengths.astype(jnp.float32))[:, None, None]
    whitened = whiten(seq_grads, cov_out / row_total, cov_in / row_total).astype(jnp.bfloat16)
    return jnp.dot(
        lax.all_gather(whitened, "rows", axis=0, tiled=True),
        grad_store.T,
        preferred_element_type=jnp.float32,
    )


LANES = 128
HIGHEST = lax.Precision.HIGHEST
MESH = pl.DeviceIdType.MESH


def dot_f32(left, right, dims):
    return lax.dot_general(
        left, right, (dims, ((), ())), precision=HIGHEST, preferred_element_type=jnp.float32
    )


def split(value):
    upper = value.astype(jnp.bfloat16)
    return upper, (value - upper.astype(jnp.float32)).astype(jnp.bfloat16)


def dot_three(left, right):
    left_upper, left_lower = split(left)
    right_upper, right_lower = split(right)
    small = jnp.dot(left_upper, right_lower, preferred_element_type=jnp.float32) + jnp.dot(
        left_lower, right_upper, preferred_element_type=jnp.float32
    )
    return small + jnp.dot(left_upper, right_upper, preferred_element_type=jnp.float32)


def damped_inverse(cov):
    width = cov.shape[0]
    identity = (
        lax.broadcasted_iota(jnp.int32, cov.shape, 0) == lax.broadcasted_iota(jnp.int32, cov.shape, 1)
    ).astype(jnp.float32)
    diagonal = jnp.sum(cov * identity, axis=0, keepdims=True)
    trace = jnp.sum(diagonal, axis=1, keepdims=True)
    damp = damping_ratio * trace / width + tiny_value
    shrink = 1.0 / (damp + 0.5 * trace)
    scaled = (cov + identity * damp) * shrink
    reach = 1.0 / (1.0 + 2.0 * damping_ratio / width)
    gain = 2.0 / (2.0 - reach * reach)
    inverse = gain * (2.0 * identity - scaled)
    reach = reach * reach / (2.0 - reach * reach)
    while reach > 1e-8:
        gain = 2.0 / (2.0 - reach * reach)
        reach = reach * reach / (2.0 - reach * reach)
        if reach > 1e-3:
            inverse = gain * (2.0 * inverse - dot_three(inverse, dot_three(scaled, inverse)))
        else:
            again = dot_f32(scaled, inverse, ((1,), (0,)))
            inverse = gain * (2.0 * inverse - dot_f32(inverse, again, ((1,), (0,))))
    return inverse * shrink


def kernel(
    line,
    parts,
    hidden_ref,
    head_ref,
    in_proj_hbm,
    out_proj_hbm,
    targets_hbm,
    lengths_hbm,
    store_ref,
    scores_ref,
    feat,
    weights,
    logits,
    inner,
    store,
    turned,
    in_proj_ref,
    out_proj_ref,
    targets_ref,
    lengths_ref,
    table,
    pick,
    pick_in,
    stat,
    stat_in,
    grad,
    grad_in,
    side_in,
    mix,
    mix_in,
    white,
    flat,
    load_sem,
    head_send,
    head_recv,
    feat_send,
    feat_recv,
    pick_sems,
    stat_sems,
    grad_sems,
    side_send,
    side_recv,
    mix_send,
    mix_recv,
):
    count = line * 4
    me = lax.axis_index("vocab")
    row = lax.axis_index("rows")
    z, y, x = me // 4, (me // 2) % 2, me % 2
    tokens, block = hidden_ref.shape
    long_rows, short_rows = class_rows(tokens)
    starts = (0, long_rows, 2 * long_rows, 2 * long_rows + short_rows)
    sizes = (long_rows, long_rows, short_rows, short_rows)
    depth, vocab_cols = head_ref.shape
    width = out_proj_ref.shape[0]
    own = tokens // count
    tiles = tokens // TILE
    seq_count = tiles * parts

    def send(source, target, send_sem, recv_sem, device):
        return pltpu.make_async_remote_copy(
            src_ref=source,
            dst_ref=target,
            send_sem=send_sem,
            recv_sem=recv_sem,
            device_id=device,
            device_id_type=MESH,
        )

    def await_bytes(ref, sem):
        pltpu.make_async_copy(ref, ref, sem).wait()

    barrier = pltpu.get_barrier_semaphore()

    def greet(step, carry):
        pl.semaphore_signal(
            barrier, inc=1, device_id={"vocab": (me + step) % count}, device_id_type=MESH
        )
        return carry

    lax.fori_loop(1, count, greet, 0)
    for step in range(1, parts):
        pl.semaphore_signal(
            barrier, inc=1, device_id={"rows": (row + step) % parts}, device_id_type=MESH
        )
    local_feat = pltpu.make_async_copy(hidden_ref, feat.at[me], load_sem.at[0])
    local_store = pltpu.make_async_copy(store_ref, store, load_sem.at[2])
    local_feat.start()
    small = [
        pltpu.make_async_copy(source, target, load_sem.at[3 + at])
        for at, (source, target) in enumerate(
            [
                (out_proj_hbm, out_proj_ref),
                (targets_hbm, targets_ref),
                (lengths_hbm, lengths_ref),
                (in_proj_hbm, in_proj_ref),
            ]
        )
    ]
    for copy in small:
        copy.start()
    chunk = 4 * block
    per_part = line // parts

    def head_chunk(zz):
        return weights.at[pl.ds(pl.multiple_of(zz * chunk, chunk), chunk)]

    for at in range(per_part):
        pltpu.make_async_copy(
            head_ref.at[pl.ds(at * chunk, chunk)],
            head_chunk(row * per_part + at),
            head_recv.at[row * per_part + at],
        ).start()
    local_store.start()
    pl.semaphore_wait(barrier, count - 1 + parts - 1)

    def place(zz, yy, xx):
        return (zz * 2 + yy) * 2 + xx

    def item(zz, side, pair):
        near, far = pair % 2, pair // 2
        flip_y, flip_x = (far, near) if side % 2 == 0 else (near, far)
        return place(zz, (y + flip_y) % 2, (x + flip_x) % 2)

    def piece(index, side):
        return feat.at[index, pl.ds(starts[side], sizes[side])]

    def hop(index, side, route, device, source=None):
        return send(
            piece(index, side) if source is None else source,
            piece(index, side),
            feat_send.at[route, side, index],
            feat_recv.at[side, index],
            {"vocab": device},
        )

    nearest = jnp.minimum(z, line - 1 - z)

    def nth(k):
        if k == 0:
            return z
        sign_near = -1 if k % 2 == 1 else 1
        sign_far = jnp.where(z < line - 1 - z, 1, -1)
        return z + jnp.where(k <= 2 * nearest, sign_near * ((k + 1) // 2), sign_far * (k - nearest))

    def own_rows_of(side):
        return hidden_ref.at[pl.ds(starts[side], sizes[side])]

    def along(k, side, pair, action, source=None):
        zz = nth(k)
        index = item(zz, side, pair)
        up = z < line - 1
        down = z > 0
        if k > 0:
            up = jnp.logical_and(zz < z, up)
            down = jnp.logical_and(zz > z, down)

        @pl.when(up)
        def _():
            action(hop(index, side, 0, place(jnp.minimum(z + 1, line - 1), y, x), source))

        @pl.when(down)
        def _():
            action(hop(index, side, 1, place(jnp.maximum(z - 1, 0), y, x), source))

    def outward(k, side, action):
        source = own_rows_of(side) if k == 0 else None
        index = item(nth(k), side, 0)
        along(k, side, 0, action, source)
        action(hop(index, side, 2, item(z, side, 1), source))
        action(hop(index, side, 3, item(z, side, 2), source))

    def onward(k, side):
        return hop(item(nth(k), side, 1), side, 2, item(z, side, 2))

    def arrived(index, side):
        hop(index, side, 0, me).wait_recv()

    strip = 2 * LANES

    def multiply(k):
        zz = nth(k)
        for pair in (2, 3):
            for side in range(2):
                arrived(item(zz, side, pair), side)
        pltpu.make_async_copy(head_chunk(zz), head_chunk(zz), head_recv.at[zz]).wait()

        def wide():
            return jnp.concatenate([feat[place(zz, at // 2, at % 2)] for at in range(4)], axis=1)

        rows = pl.ds(pl.multiple_of(zz * chunk, chunk), chunk)

        def body(step, carry):
            columns = pl.ds(pl.multiple_of(step * strip, strip), strip)
            product = jnp.dot(wide(), weights[rows, columns], preferred_element_type=jnp.float32)
            logits[:, columns] = product if k == 0 else logits[:, columns] + product
            return carry

        lax.fori_loop(0, vocab_cols // strip, body, 0)
        product = lax.dot_general(
            wide(), in_proj_ref[:, rows], (((1,), (1,)), ((), ())), preferred_element_type=jnp.float32
        )
        inner[...] = product if k == 0 else inner[...] + product

    def short_arrivals(k):
        for pair in range(4):
            for side in (2, 3):
                if k > 0:
                    arrived(item(nth(k), side, pair), side)
                    along(k, side, pair, lambda copy: copy.start())

    def short_start(side, action):
        source = own_rows_of(side)
        action(hop(me, side, 2, item(z, side, 1), source))
        action(hop(me, side, 3, item(z, side, 2), source))
        along(0, side, 0, action, source)

    def short_onward(pair, side, action):
        index = item(z, side, pair)
        if pair == 1:
            action(hop(index, side, 2, item(z, side, 2)))
        along(0, side, pair, action)

    for side in (2, 3):
        short_start(side, lambda copy: copy.start())
    for side in range(2):
        outward(0, side, lambda copy: copy.start())
    def head_copy(k, step):
        zz = nth(k)
        at = zz % per_part
        return send(
            head_ref.at[pl.ds(pl.multiple_of(at * chunk, chunk), chunk)],
            head_chunk(zz),
            head_send.at[step, zz],
            head_recv.at[zz],
            {"rows": (row + step) % parts},
        )

    def head_sends(action):
        for k in range(line):

            @pl.when(nth(k) // per_part == row)
            def _():
                for step in range(1, parts):
                    action(head_copy(k, step))

    head_sends(lambda copy: copy.start())

    for copy in small:
        copy.wait()
    marker = lax.broadcasted_iota(jnp.int32, (LANES - width, vocab_cols), 0)
    upright = jnp.concatenate([out_proj_ref[...].astype(jnp.float32), (marker == 0).astype(jnp.float32)], axis=0)
    table[...] = upright.T.astype(jnp.bfloat16)
    column_ids = lax.broadcasted_iota(jnp.int32, (vocab_cols, tokens), 0) + me * vocab_cols
    onehot = (column_ids == targets_ref[...]).astype(jnp.float32).astype(jnp.bfloat16)
    pick[...] = jnp.dot(
        upright.astype(jnp.bfloat16), onehot, preferred_element_type=jnp.float32
    ).T.astype(jnp.bfloat16)

    def own_part(ref, device):
        return ref.at[pl.ds(pl.multiple_of(device * own, own), own)]

    def slot(device):
        return (me - device - 1 + 2 * count) % count

    def send_pick(step, carry):
        device = (me + step) % count
        send(
            own_part(pick, device),
            pick_in.at[slot(device)],
            pick_sems.at[0],
            pick_sems.at[1],
            {"vocab": device},
        ).start()
        return carry

    lax.fori_loop(1, count, send_pick, 0)

    for k in range(line):
        if k == 1:
            for pair in (1, 2, 3):
                for side in (2, 3):
                    arrived(item(z, side, pair), side)
                    short_onward(pair, side, lambda copy: copy.start())
        if k > 0:
            for side in range(2):
                arrived(place(nth(k), y, x), side)
                outward(k, side, lambda copy: copy.start())
            for side in range(2):
                arrived(item(nth(k - 1), side, 1), side)
                onward(k - 1, side).start()
            short_arrivals(k - 1)
        if k == 1:
            local_feat.wait()
        if k == 1:
            local_store.wait()
            turned_columns = 4 * LANES

            def turn(step, carry):
                columns = pl.ds(pl.multiple_of(step * turned_columns, turned_columns), turned_columns)
                turned[columns, :] = store[:, columns].astype(jnp.float32).T.astype(jnp.bfloat16)
                return carry

            lax.fori_loop(0, width * width // turned_columns, turn, 0)
        if k > 1:
            multiply(k - 2)
    for side in range(2):
        arrived(item(nth(line - 1), side, 1), side)
        onward(line - 1, side).start()
    multiply(line - 2)
    short_arrivals(line - 1)
    multiply(line - 1)

    lanes = lax.broadcasted_iota(jnp.int32, (TILE, LANES), 1)
    per_tile = TILE // own
    for tile in range(tiles):
        part = logits[tile * TILE : (tile + 1) * TILE, :]
        top = jnp.max(part, axis=1, keepdims=True)
        exponent = jnp.exp(part - top)
        upper = exponent.astype(jnp.bfloat16)
        lower = (exponent - upper.astype(jnp.float32)).astype(jnp.bfloat16)
        weighted = jnp.dot(upper, table[...], preferred_element_type=jnp.float32) + jnp.dot(
            lower, table[...], preferred_element_type=jnp.float32
        )
        stat[tile * TILE : (tile + 1) * TILE, :] = jnp.where(lanes == width + 1, top, weighted)
        for device in range(tile * per_tile, (tile + 1) * per_tile):

            @pl.when(me != device)
            def _():
                send(
                    stat.at[pl.ds(device * own, own)],
                    stat_in.at[slot(device)],
                    stat_sems.at[0],
                    stat_sems.at[1],
                    {"vocab": device},
                ).start()

    position = lax.broadcasted_iota(jnp.int32, (TILE, LANES), 0)
    masked_in = []
    for tile in range(tiles):
        valid = (position < lengths_ref[row * tiles + tile]).astype(jnp.float32)
        masked_in.append(inner[tile * TILE : (tile + 1) * TILE, :] * valid[:, :width])
    flat_in = jnp.concatenate(masked_in, axis=0)
    side_in[row] = dot_f32(flat_in, flat_in, ((0,), (0,)))
    side_copies = []
    for step in range(1, parts):
        copy = send(
            side_in.at[row], side_in.at[row], side_send.at[step], side_recv.at[row], {"rows": (row + step) % parts}
        )
        copy.start()
        side_copies.append(copy)
    row_total = lengths_ref[0]
    for sequence in range(1, seq_count):
        row_total = row_total + lengths_ref[sequence]
    one_over = 1.0 / jnp.full((1, width), row_total, jnp.int32).astype(jnp.float32)
    for k in range(line):
        for side in range(2):
            outward(k, side, lambda copy: copy.wait_send())
            onward(k, side).wait_send()
        for side in (2, 3):
            for pair in range(4):
                if k > 0:
                    along(k, side, pair, lambda copy: copy.wait_send())
                elif pair > 0:
                    short_onward(pair, side, lambda copy: copy.wait_send())
                else:
                    short_start(side, lambda copy: copy.wait_send())
    head_sends(lambda copy: copy.wait_send())
    for step in range(1, parts):
        other = (row + step) % parts
        send(side_in.at[row], side_in.at[other], side_send.at[0], side_recv.at[other], {"rows": row}).wait_recv()
    cov_in = side_in[0]
    for part in range(1, parts):
        cov_in = cov_in + side_in[part]
    inverse_in = damped_inverse(cov_in * one_over)
    flat_in = dot_three(flat_in, inverse_in)

    await_bytes(pick_in, pick_sems.at[1])
    picked = own_part(pick, me)[...].astype(jnp.float32)
    for other in range(count - 1):
        picked = picked + pick_in[other].astype(jnp.float32)
    await_bytes(stat_in, stat_sems.at[1])
    mine = own_part(stat, me)[...]
    tops = [mine[:, width + 1 : width + 2]]
    for other in range(count - 1):
        tops.append(stat_in[other][:, width + 1 : width + 2])
    joint = functools.reduce(jnp.maximum, tops)
    total = mine * jnp.exp(tops[0] - joint)
    for other in range(count - 1):
        total = total + stat_in[other] * jnp.exp(tops[other + 1] - joint)
    first = me * own
    place_in_tile = lax.broadcasted_iota(jnp.int32, (own, LANES), 0) + first % TILE
    valid = (place_in_tile < lengths_ref[row * tiles + first // TILE]).astype(jnp.float32)
    finished = (total / total[:, width : width + 1] - picked) * valid
    grad[...] = jnp.concatenate([finished[: own // 2, :width], finished[own // 2 :, :width]], axis=1)

    def send_grad(step, carry):
        device = (me + step) % count
        send(grad, grad_in.at[me], grad_sems.at[0], grad_sems.at[1], {"vocab": device}).start()
        return carry

    lax.fori_loop(1, count, send_grad, 0)
    grad_in[me] = grad[...]
    await_bytes(grad_in.at[pl.ds(0, count - 1)], grad_sems.at[1])

    for tile in range(tiles):
        pieces = []
        for other in range(tile * per_tile, (tile + 1) * per_tile):
            pieces += [grad_in[other][:, :width], grad_in[other][:, width:]]
        grads = jnp.concatenate(pieces, axis=0)
        joined_sides = jnp.concatenate([grads, flat_in[tile * TILE : (tile + 1) * TILE, :]], axis=1)
        mix[row, tile] = dot_f32(grads, joined_sides, ((0,), (0,)))
    mix_copies = []
    for step in range(1, parts):
        copy = send(
            mix.at[row], mix_in.at[row], mix_send.at[step], mix_recv.at[row], {"rows": (row + step) % parts}
        )
        copy.start()
        mix_copies.append(copy)
    mix_in[row] = mix[row]
    for step in range(1, parts):
        other = (row + step) % parts
        send(mix.at[row], mix_in.at[other], mix_send.at[0], mix_recv.at[other], {"rows": row}).wait_recv()

    cov_out = jnp.zeros((width, LANES), jnp.float32)
    stacked = []
    for part in range(parts):
        for tile in range(tiles):
            block_mix = mix_in[part, tile]
            cov_out = cov_out + block_mix
            long = jnp.full((1, LANES), lengths_ref[part * tiles + tile], jnp.int32)
            stacked.append(block_mix * lax.rsqrt(long.astype(jnp.float32)))
    inverse_out = damped_inverse(cov_out[:, :width] * one_over)
    whitened = dot_three(inverse_out, jnp.concatenate(stacked, axis=1))
    for sequence in range(seq_count):
        white[sequence * width : (sequence + 1) * width, :] = whitened[
            :, sequence * LANES : (sequence + 1) * LANES
        ]
    for pair in range(width // 2):
        even = white[pl.ds(2 * pair, seq_count, stride=width), :]
        odd = white[pl.ds(2 * pair + 1, seq_count, stride=width), :]
        flat[:, pair * LANES : (pair + 1) * LANES] = jnp.concatenate(
            [even[:, width:], odd[:, width:]], axis=1
        )
    scores_ref[...] = jnp.dot(
        flat[...].astype(jnp.bfloat16), turned[...], preferred_element_type=jnp.float32
    )

    for copy in side_copies + mix_copies:
        copy.wait_send()
    await_bytes(pick_in, pick_sems.at[0])
    await_bytes(stat_in, stat_sems.at[0])
    await_bytes(grad_in.at[pl.ds(0, count - 1)], grad_sems.at[0])


def class_rows(tokens):
    short = tokens // 10 // 16 * 16
    return tokens // 2 - short, short


def per_device_any(count, parts, hidden, head_weight, in_proj, out_proj, targets, lengths, grad_store):
    tokens, block = hidden.shape
    vocab_cols = head_weight.shape[1]
    width = in_proj.shape[1]
    own = tokens // count
    tiles = tokens // TILE
    fits = (
        count % (4 * parts) == 0
        and block % LANES == 0
        and 2 * width == LANES
        and own % 32 == 0
        and tokens % 32 == 0
        and tokens >= 160
        and TILE % own == 0
        and grad_store.shape[1] == width * width
        and width * width % (4 * LANES) == 0
        and vocab_cols % (2 * LANES) == 0
    )
    if not fits:
        return per_device(hidden, head_weight, in_proj, out_proj, targets, lengths, grad_store)
    line = count // 4
    seq_count = lengths.shape[0]
    hbm = pl.BlockSpec(memory_space=pltpu.HBM)
    vmem = pl.BlockSpec(memory_space=pltpu.VMEM)
    dma = pltpu.SemaphoreType.DMA
    f32, bf16 = jnp.float32, jnp.bfloat16
    return pl.pallas_call(
        functools.partial(kernel, line, parts),
        out_shape=jax.ShapeDtypeStruct((seq_count, grad_store.shape[0]), f32),
        in_specs=[hbm] * 7,
        out_specs=vmem,
        scratch_shapes=[
            pltpu.VMEM((count, tokens, block), bf16),
            pltpu.VMEM((head_weight.shape[0] * parts, vocab_cols), bf16),
            pltpu.VMEM((tokens, vocab_cols), f32),
            pltpu.VMEM((tokens, width), f32),
            pltpu.VMEM(grad_store.shape, bf16),
            pltpu.VMEM(grad_store.shape[::-1], bf16),
            pltpu.VMEM(in_proj.shape[::-1], bf16),
            pltpu.VMEM(out_proj.shape[::-1], bf16),
            pltpu.VMEM((1, tokens), jnp.int32),
            pltpu.SMEM(lengths.shape, jnp.int32),
            pltpu.VMEM((vocab_cols, LANES), bf16),
            pltpu.VMEM((tokens, LANES), bf16),
            pltpu.VMEM((count - 1, own, LANES), bf16),
            pltpu.VMEM((tokens, LANES), f32),
            pltpu.VMEM((count - 1, own, LANES), f32),
            pltpu.VMEM((own // 2, LANES), f32),
            pltpu.VMEM((count, own // 2, LANES), f32),
            pltpu.VMEM((parts, width, width), f32),
            pltpu.VMEM((parts, tiles, width, LANES), f32),
            pltpu.VMEM((parts, tiles, width, LANES), f32),
            pltpu.VMEM((seq_count * width, LANES), f32),
            pltpu.VMEM((seq_count, width * width), f32),
            dma((7,)),
            dma((parts, line)),
            dma((line,)),
            dma((4, 4, count)),
            dma((4, count)),
            dma((2,)),
            dma((2,)),
            dma((2,)),
            dma((parts,)),
            dma((parts,)),
            dma((parts,)),
            dma((parts,)),
        ],
        compiler_params=pltpu.CompilerParams(
            collective_id=0, has_side_effects=True, vmem_limit_bytes=64 * 1024 * 1024
        ),
        cost_estimate=pl.CostEstimate(
            flops=2 * tokens * block * count * vocab_cols,
            bytes_accessed=4 * tokens * block * count,
            transcendentals=tokens * vocab_cols,
        ),
    )(hidden, head_weight, in_proj.T, out_proj.T, targets[None, :], lengths, grad_store)


def solution(mesh):
    return jax.shard_map(
        functools.partial(per_device_any, mesh.shape["vocab"], mesh.shape["rows"]),
        mesh=mesh,
        in_specs=(
            P("rows", "vocab"),
            P("rows", "vocab"),
            P(),
            P("vocab", None),
            P("rows"),
            P(),
            P(("vocab", "rows"), None),
        ),
        out_specs=P(None, ("vocab", "rows")),
        check_vma=False,
    )
```

```python
import functools

import jax
import jax.numpy as jnp
from jax import lax
from jax.experimental import pallas as pl
from jax.experimental.pallas import tpu as pltpu
from jax.sharding import PartitionSpec as P

TILE = 128


damping_ratio = 0.1
tiny_value = 1e-06


def joined(value, axis, join):
    pieces = jax.tree.map(lambda part: lax.all_gather(part, axis), value)
    head = jax.tree.map(lambda part: part[0], pieces)
    tail = jax.tree.map(lambda part: part[1:], pieces)
    running, _ = lax.scan(lambda running, slab: (join(running, slab), None), head, tail)
    return running


def whiten(seq_grads, cov_out, cov_in):
    proj_width = cov_out.shape[0]
    seq_count = seq_grads.shape[0]
    identity = jnp.eye(proj_width, dtype=jnp.float32)
    damp_out = damping_ratio * jnp.trace(cov_out) / proj_width + tiny_value
    damp_in = damping_ratio * jnp.trace(cov_in) / proj_width + tiny_value
    lower_out = jnp.linalg.cholesky(cov_out + damp_out * identity)
    lower_in = jnp.linalg.cholesky(cov_in + damp_in * identity)
    stacked = jnp.transpose(seq_grads, (1, 0, 2)).reshape(proj_width, seq_count * proj_width)
    left_half = lax.linalg.triangular_solve(lower_out, stacked, left_side=True, lower=True)
    left_full = lax.linalg.triangular_solve(
        lower_out, left_half, left_side=True, lower=True, transpose_a=True
    )
    rows_form = jnp.transpose(
        left_full.reshape(proj_width, seq_count, proj_width), (1, 0, 2)
    ).reshape(seq_count * proj_width, proj_width)
    right_half = lax.linalg.triangular_solve(
        lower_in, rows_form, left_side=False, lower=True, transpose_a=True
    )
    right_full = lax.linalg.triangular_solve(lower_in, right_half, left_side=False, lower=True)
    return right_full.reshape(seq_count, proj_width * proj_width)


def combine_rows(earlier, later):
    max_one, sum_one, weight_one = earlier
    max_two, sum_two, weight_two = later
    joint_max = jnp.maximum(max_one, max_two)
    scale_one = jnp.exp(max_one - joint_max)
    scale_two = jnp.exp(max_two - joint_max)
    joint_sum = sum_one * scale_one + sum_two * scale_two
    joint_weight = weight_one * scale_one[:, None] + weight_two * scale_two[:, None]
    return (joint_max, joint_sum, joint_weight)


def per_device(hidden, head_weight, in_proj, out_proj, targets, lengths, grad_store):
    token_count = hidden.shape[0]
    vocab_cols = head_weight.shape[1]
    proj_width = in_proj.shape[1]
    tile_count = token_count // TILE
    features = lax.all_gather(hidden, "vocab", axis=1, tiled=True)
    out_table = out_proj.astype(jnp.float32)
    first_column = lax.axis_index("vocab") * vocab_cols
    column_ids = lax.broadcasted_iota(jnp.int32, (token_count, vocab_cols), 1) + first_column
    onehot = (column_ids == targets[:, None]).astype(jnp.float32)
    picked_local = jnp.dot(onehot, out_table, precision=lax.Precision.HIGHEST)
    picked = lax.psum(picked_local, "vocab")
    logits = jnp.dot(
        features,
        lax.all_gather(head_weight, "rows", axis=0, tiled=True),
        preferred_element_type=jnp.float32,
    )
    local_max = jnp.max(logits, axis=1)
    exponent = jnp.exp(logits - local_max[:, None])
    weighted = jnp.dot(exponent, out_table, precision=lax.Precision.HIGHEST)
    merged = joined((local_max, jnp.sum(exponent, axis=1), weighted), "vocab", combine_rows)
    out_grad = merged[2] / merged[1][:, None] - picked
    input_proj = jnp.dot(features, in_proj, preferred_element_type=jnp.float32)
    own_lengths = lax.dynamic_slice_in_dim(lengths, lax.axis_index("rows") * tile_count, tile_count)
    position = lax.broadcasted_iota(jnp.int32, (tile_count, TILE), 1)
    is_valid = (position < own_lengths[:, None]).astype(jnp.float32)[:, :, None]
    out_tiles = out_grad.reshape(tile_count, TILE, proj_width) * is_valid
    in_tiles = input_proj.reshape(tile_count, TILE, proj_width) * is_valid
    flat_out = out_tiles.reshape(token_count, proj_width)
    flat_in = in_tiles.reshape(token_count, proj_width)
    local_out = jnp.dot(flat_out.T, flat_out, precision=lax.Precision.HIGHEST)
    local_in = jnp.dot(flat_in.T, flat_in, precision=lax.Precision.HIGHEST)
    cov_out, cov_in = lax.psum((local_out, local_in), "rows")
    row_total = jnp.sum(lengths).astype(jnp.float32)
    seq_grads = jnp.einsum("stk,stj->skj", out_tiles, in_tiles, precision=lax.Precision.HIGHEST)
    seq_grads = seq_grads / jnp.sqrt(own_lengths.astype(jnp.float32))[:, None, None]
    whitened = whiten(seq_grads, cov_out / row_total, cov_in / row_total).astype(jnp.bfloat16)
    return jnp.dot(
        lax.all_gather(whitened, "rows", axis=0, tiled=True),
        grad_store.T,
        preferred_element_type=jnp.float32,
    )


LANES = 128
HIGHEST = lax.Precision.HIGHEST
MESH = pl.DeviceIdType.MESH


def dot_f32(left, right, dims):
    return lax.dot_general(
        left, right, (dims, ((), ())), precision=HIGHEST, preferred_element_type=jnp.float32
    )


def split(value):
    upper = value.astype(jnp.bfloat16)
    return upper, (value - upper.astype(jnp.float32)).astype(jnp.bfloat16)


def dot_three(left, right):
    left_upper, left_lower = split(left)
    right_upper, right_lower = split(right)
    small = jnp.dot(left_upper, right_lower, preferred_element_type=jnp.float32) + jnp.dot(
        left_lower, right_upper, preferred_element_type=jnp.float32
    )
    return small + jnp.dot(left_upper, right_upper, preferred_element_type=jnp.float32)


def damped_inverse(cov):
    width = cov.shape[0]
    identity = (
        lax.broadcasted_iota(jnp.int32, cov.shape, 0) == lax.broadcasted_iota(jnp.int32, cov.shape, 1)
    ).astype(jnp.float32)
    diagonal = jnp.sum(cov * identity, axis=0, keepdims=True)
    trace = jnp.sum(diagonal, axis=1, keepdims=True)
    damp = damping_ratio * trace / width + tiny_value
    shrink = 1.0 / (damp + 0.5 * trace)
    scaled = (cov + identity * damp) * shrink
    reach = 1.0 / (1.0 + 2.0 * damping_ratio / width)
    gain = 2.0 / (2.0 - reach * reach)
    error = identity - scaled
    inverse = gain * (identity + error)
    error = (1.0 - gain) * identity + gain * dot_f32(error, error, ((1,), (0,)))
    reach = reach * reach / (2.0 - reach * reach)
    while reach > 1e-8:
        gain = 2.0 / (2.0 - reach * reach)
        reach = reach * reach / (2.0 - reach * reach)
        if reach > 1e-8:
            inverse = gain * (inverse + dot_f32(inverse, error, ((1,), (0,))))
            error = (1.0 - gain) * identity + gain * dot_f32(error, error, ((1,), (0,)))
        else:
            again = dot_f32(scaled, inverse, ((1,), (0,)))
            inverse = gain * (2.0 * inverse - dot_f32(inverse, again, ((1,), (0,))))
    return inverse * shrink


def kernel(
    line,
    parts,
    hidden_ref,
    head_ref,
    in_proj_hbm,
    out_proj_hbm,
    targets_hbm,
    lengths_hbm,
    store_ref,
    scores_ref,
    feat,
    weights,
    logits,
    inner,
    store,
    turned,
    in_proj_ref,
    out_proj_ref,
    targets_ref,
    lengths_ref,
    table,
    pick,
    pick_in,
    stat,
    stat_in,
    grad,
    grad_in,
    side_in,
    mix,
    mix_in,
    white,
    flat,
    load_sem,
    head_send,
    head_recv,
    feat_send,
    feat_recv,
    pick_sems,
    stat_sems,
    grad_sems,
    side_send,
    side_recv,
    mix_send,
    mix_recv,
):
    count = line * 4
    me = lax.axis_index("vocab")
    row = lax.axis_index("rows")
    z, y, x = me // 4, (me // 2) % 2, me % 2
    tokens, block = hidden_ref.shape
    long_rows, short_rows = class_rows(tokens)
    starts = (0, long_rows, 2 * long_rows, 2 * long_rows + short_rows)
    sizes = (long_rows, long_rows, short_rows, short_rows)
    depth, vocab_cols = head_ref.shape
    width = out_proj_ref.shape[0]
    own = tokens // count
    tiles = tokens // TILE
    seq_count = tiles * parts

    def send(source, target, send_sem, recv_sem, device):
        return pltpu.make_async_remote_copy(
            src_ref=source,
            dst_ref=target,
            send_sem=send_sem,
            recv_sem=recv_sem,
            device_id=device,
            device_id_type=MESH,
        )

    def await_bytes(ref, sem):
        pltpu.make_async_copy(ref, ref, sem).wait()

    barrier = pltpu.get_barrier_semaphore()

    def greet(step, carry):
        pl.semaphore_signal(
            barrier, inc=1, device_id={"vocab": (me + step) % count}, device_id_type=MESH
        )
        return carry

    lax.fori_loop(1, count, greet, 0)
    for step in range(1, parts):
        pl.semaphore_signal(
            barrier, inc=1, device_id={"rows": (row + step) % parts}, device_id_type=MESH
        )
    local_feat = pltpu.make_async_copy(hidden_ref, feat.at[me], load_sem.at[0])
    local_store = pltpu.make_async_copy(store_ref, store, load_sem.at[2])
    local_feat.start()
    small = [
        pltpu.make_async_copy(source, target, load_sem.at[3 + at])
        for at, (source, target) in enumerate(
            [
                (out_proj_hbm, out_proj_ref),
                (targets_hbm, targets_ref),
                (lengths_hbm, lengths_ref),
                (in_proj_hbm, in_proj_ref),
            ]
        )
    ]
    for copy in small:
        copy.start()
    chunk = 4 * block
    per_part = line // parts

    def head_chunk(zz):
        return weights.at[pl.ds(pl.multiple_of(zz * chunk, chunk), chunk)]

    for at in range(per_part):
        pltpu.make_async_copy(
            head_ref.at[pl.ds(at * chunk, chunk)],
            head_chunk(row * per_part + at),
            head_recv.at[row * per_part + at],
        ).start()
    local_store.start()
    pl.semaphore_wait(barrier, count - 1 + parts - 1)

    def place(zz, yy, xx):
        return (zz * 2 + yy) * 2 + xx

    def item(zz, side, pair):
        near, far = pair % 2, pair // 2
        flip_y, flip_x = (far, near) if side % 2 == 0 else (near, far)
        return place(zz, (y + flip_y) % 2, (x + flip_x) % 2)

    def piece(index, side):
        return feat.at[index, pl.ds(starts[side], sizes[side])]

    def hop(index, side, route, device, source=None):
        return send(
            piece(index, side) if source is None else source,
            piece(index, side),
            feat_send.at[route, side, index],
            feat_recv.at[side, index],
            {"vocab": device},
        )

    nearest = jnp.minimum(z, line - 1 - z)

    def nth(k):
        if k == 0:
            return z
        sign_near = -1 if k % 2 == 1 else 1
        sign_far = jnp.where(z < line - 1 - z, 1, -1)
        return z + jnp.where(k <= 2 * nearest, sign_near * ((k + 1) // 2), sign_far * (k - nearest))

    def own_rows_of(side):
        return hidden_ref.at[pl.ds(starts[side], sizes[side])]

    def along(k, side, pair, action, source=None):
        zz = nth(k)
        index = item(zz, side, pair)
        up = z < line - 1
        down = z > 0
        if k > 0:
            up = jnp.logical_and(zz < z, up)
            down = jnp.logical_and(zz > z, down)

        @pl.when(up)
        def _():
            action(hop(index, side, 0, place(jnp.minimum(z + 1, line - 1), y, x), source))

        @pl.when(down)
        def _():
            action(hop(index, side, 1, place(jnp.maximum(z - 1, 0), y, x), source))

    def outward(k, side, action):
        source = own_rows_of(side) if k == 0 else None
        index = item(nth(k), side, 0)
        along(k, side, 0, action, source)
        action(hop(index, side, 2, item(z, side, 1), source))
        action(hop(index, side, 3, item(z, side, 2), source))

    def onward(k, side):
        return hop(item(nth(k), side, 1), side, 2, item(z, side, 2))

    def arrived(index, side):
        hop(index, side, 0, me).wait_recv()

    strip = 2 * LANES

    def multiply(k):
        zz = nth(k)
        for pair in (2, 3):
            for side in range(2):
                arrived(item(zz, side, pair), side)
        pltpu.make_async_copy(head_chunk(zz), head_chunk(zz), head_recv.at[zz]).wait()

        def wide():
            return jnp.concatenate([feat[place(zz, at // 2, at % 2)] for at in range(4)], axis=1)

        rows = pl.ds(pl.multiple_of(zz * chunk, chunk), chunk)

        def body(step, carry):
            columns = pl.ds(pl.multiple_of(step * strip, strip), strip)
            product = jnp.dot(wide(), weights[rows, columns], preferred_element_type=jnp.float32)
            logits[:, columns] = product if k == 0 else logits[:, columns] + product
            return carry

        lax.fori_loop(0, vocab_cols // strip, body, 0)
        product = lax.dot_general(
            wide(), in_proj_ref[:, rows], (((1,), (1,)), ((), ())), preferred_element_type=jnp.float32
        )
        inner[...] = product if k == 0 else inner[...] + product

    def short_arrivals(k):
        for pair in range(4):
            for side in (2, 3):
                if k > 0:
                    arrived(item(nth(k), side, pair), side)
                    along(k, side, pair, lambda copy: copy.start())

    def short_start(side, action):
        source = own_rows_of(side)
        action(hop(me, side, 2, item(z, side, 1), source))
        action(hop(me, side, 3, item(z, side, 2), source))
        along(0, side, 0, action, source)

    def short_onward(pair, side, action):
        index = item(z, side, pair)
        if pair == 1:
            action(hop(index, side, 2, item(z, side, 2)))
        along(0, side, pair, action)

    for side in (2, 3):
        short_start(side, lambda copy: copy.start())
    for side in range(2):
        outward(0, side, lambda copy: copy.start())
    def head_copy(k, step):
        zz = nth(k)
        at = zz % per_part
        return send(
            head_ref.at[pl.ds(pl.multiple_of(at * chunk, chunk), chunk)],
            head_chunk(zz),
            head_send.at[step, zz],
            head_recv.at[zz],
            {"rows": (row + step) % parts},
        )

    def head_sends(action):
        for k in range(line):

            @pl.when(nth(k) // per_part == row)
            def _():
                for step in range(1, parts):
                    action(head_copy(k, step))

    head_sends(lambda copy: copy.start())

    def own_part(ref, device):
        return ref.at[pl.ds(pl.multiple_of(device * own, own), own)]

    def slot(device):
        return (me - device - 1 + 2 * count) % count

    def send_targets():
        for copy in small:
            copy.wait()
        marker = lax.broadcasted_iota(jnp.int32, (LANES - width, vocab_cols), 0)
        upright = jnp.concatenate([out_proj_ref[...].astype(jnp.float32), (marker == 0).astype(jnp.float32)], axis=0)
        table[...] = upright.T.astype(jnp.bfloat16)
        column_ids = lax.broadcasted_iota(jnp.int32, (vocab_cols, tokens), 0) + me * vocab_cols
        onehot = (column_ids == targets_ref[...]).astype(jnp.float32).astype(jnp.bfloat16)
        pick[...] = jnp.dot(
            upright.astype(jnp.bfloat16), onehot, preferred_element_type=jnp.float32
        ).T.astype(jnp.bfloat16)

        def send_pick(step, carry):
            device = (me + step) % count
            send(
                own_part(pick, device),
                pick_in.at[slot(device)],
                pick_sems.at[0],
                pick_sems.at[1],
                {"vocab": device},
            ).start()
            return carry

        lax.fori_loop(1, count, send_pick, 0)

    def turn_store():
        local_store.wait()
        turned_columns = 4 * LANES

        def turn(step, carry):
            columns = pl.ds(pl.multiple_of(step * turned_columns, turned_columns), turned_columns)
            turned[columns, :] = store[:, columns].astype(jnp.float32).T.astype(jnp.bfloat16)
            return carry

        lax.fori_loop(0, width * width // turned_columns, turn, 0)

    for pair in (1, 2, 3):
        for side in (2, 3):
            arrived(item(z, side, pair), side)
            short_onward(pair, side, lambda copy: copy.start())
    for k in range(1, line):
        for side in range(2):
            arrived(place(nth(k), y, x), side)
            outward(k, side, lambda copy: copy.start())
        for side in range(2):
            arrived(item(nth(k - 1), side, 1), side)
            onward(k - 1, side).start()
        if k > 1:
            short_arrivals(k - 1)
        if k == 1:
            send_targets()
    for side in range(2):
        arrived(item(nth(line - 1), side, 1), side)
        onward(line - 1, side).start()
    short_arrivals(line - 1)
    local_feat.wait()
    turn_store()
    for k in range(line):
        multiply(k)

    lanes = lax.broadcasted_iota(jnp.int32, (TILE, LANES), 1)
    per_tile = TILE // own
    for tile in range(tiles):
        part = logits[tile * TILE : (tile + 1) * TILE, :]
        top = jnp.max(part, axis=1, keepdims=True)
        exponent = jnp.exp(part - top)
        upper = exponent.astype(jnp.bfloat16)
        lower = (exponent - upper.astype(jnp.float32)).astype(jnp.bfloat16)
        weighted = jnp.dot(upper, table[...], preferred_element_type=jnp.float32) + jnp.dot(
            lower, table[...], preferred_element_type=jnp.float32
        )
        stat[tile * TILE : (tile + 1) * TILE, :] = jnp.where(lanes == width + 1, top, weighted)
        for device in range(tile * per_tile, (tile + 1) * per_tile):

            @pl.when(me != device)
            def _():
                send(
                    stat.at[pl.ds(device * own, own)],
                    stat_in.at[slot(device)],
                    stat_sems.at[0],
                    stat_sems.at[1],
                    {"vocab": device},
                ).start()

    position = lax.broadcasted_iota(jnp.int32, (TILE, LANES), 0)
    masked_in = []
    for tile in range(tiles):
        valid = (position < lengths_ref[row * tiles + tile]).astype(jnp.float32)
        masked_in.append(inner[tile * TILE : (tile + 1) * TILE, :] * valid[:, :width])
    flat_in = jnp.concatenate(masked_in, axis=0)
    side_in[row] = dot_f32(flat_in, flat_in, ((0,), (0,)))
    side_copies = []
    for step in range(1, parts):
        copy = send(
            side_in.at[row], side_in.at[row], side_send.at[step], side_recv.at[row], {"rows": (row + step) % parts}
        )
        copy.start()
        side_copies.append(copy)
    row_total = lengths_ref[0]
    for sequence in range(1, seq_count):
        row_total = row_total + lengths_ref[sequence]
    one_over = 1.0 / jnp.full((1, width), row_total, jnp.int32).astype(jnp.float32)
    for k in range(line):
        for side in range(2):
            outward(k, side, lambda copy: copy.wait_send())
            onward(k, side).wait_send()
        for side in (2, 3):
            for pair in range(4):
                if k > 0:
                    along(k, side, pair, lambda copy: copy.wait_send())
                elif pair > 0:
                    short_onward(pair, side, lambda copy: copy.wait_send())
                else:
                    short_start(side, lambda copy: copy.wait_send())
    head_sends(lambda copy: copy.wait_send())
    for step in range(1, parts):
        other = (row + step) % parts
        send(side_in.at[row], side_in.at[other], side_send.at[0], side_recv.at[other], {"rows": row}).wait_recv()
    cov_in = side_in[0]
    for part in range(1, parts):
        cov_in = cov_in + side_in[part]
    inverse_in = damped_inverse(cov_in * one_over)
    flat_in = dot_three(flat_in, inverse_in)

    await_bytes(pick_in, pick_sems.at[1])
    picked = own_part(pick, me)[...].astype(jnp.float32)
    for other in range(count - 1):
        picked = picked + pick_in[other].astype(jnp.float32)
    await_bytes(stat_in, stat_sems.at[1])
    mine = own_part(stat, me)[...]
    tops = [mine[:, width + 1 : width + 2]]
    for other in range(count - 1):
        tops.append(stat_in[other][:, width + 1 : width + 2])
    joint = functools.reduce(jnp.maximum, tops)
    total = mine * jnp.exp(tops[0] - joint)
    for other in range(count - 1):
        total = total + stat_in[other] * jnp.exp(tops[other + 1] - joint)
    first = me * own
    place_in_tile = lax.broadcasted_iota(jnp.int32, (own, LANES), 0) + first % TILE
    valid = (place_in_tile < lengths_ref[row * tiles + first // TILE]).astype(jnp.float32)
    finished = (total / total[:, width : width + 1] - picked) * valid
    grad[...] = jnp.concatenate([finished[: own // 2, :width], finished[own // 2 :, :width]], axis=1)

    def send_grad(step, carry):
        device = (me + step) % count
        send(grad, grad_in.at[me], grad_sems.at[0], grad_sems.at[1], {"vocab": device}).start()
        return carry

    lax.fori_loop(1, count, send_grad, 0)
    grad_in[me] = grad[...]
    await_bytes(grad_in.at[pl.ds(0, count - 1)], grad_sems.at[1])

    for tile in range(tiles):
        pieces = []
        for other in range(tile * per_tile, (tile + 1) * per_tile):
            pieces += [grad_in[other][:, :width], grad_in[other][:, width:]]
        grads = jnp.concatenate(pieces, axis=0)
        joined_sides = jnp.concatenate([grads, flat_in[tile * TILE : (tile + 1) * TILE, :]], axis=1)
        mix[row, tile] = dot_f32(grads, joined_sides, ((0,), (0,)))
    mix_copies = []
    for step in range(1, parts):
        copy = send(
            mix.at[row], mix_in.at[row], mix_send.at[step], mix_recv.at[row], {"rows": (row + step) % parts}
        )
        copy.start()
        mix_copies.append(copy)
    mix_in[row] = mix[row]
    for step in range(1, parts):
        other = (row + step) % parts
        send(mix.at[row], mix_in.at[other], mix_send.at[0], mix_recv.at[other], {"rows": row}).wait_recv()

    cov_out = jnp.zeros((width, LANES), jnp.float32)
    stacked = []
    for part in range(parts):
        for tile in range(tiles):
            block_mix = mix_in[part, tile]
            cov_out = cov_out + block_mix
            long = jnp.full((1, LANES), lengths_ref[part * tiles + tile], jnp.int32)
            stacked.append(block_mix * lax.rsqrt(long.astype(jnp.float32)))
    inverse_out = damped_inverse(cov_out[:, :width] * one_over)
    whitened = dot_three(inverse_out, jnp.concatenate(stacked, axis=1))
    for sequence in range(seq_count):
        white[sequence * width : (sequence + 1) * width, :] = whitened[
            :, sequence * LANES : (sequence + 1) * LANES
        ]
    for pair in range(width // 2):
        even = white[pl.ds(2 * pair, seq_count, stride=width), :]
        odd = white[pl.ds(2 * pair + 1, seq_count, stride=width), :]
        flat[:, pair * LANES : (pair + 1) * LANES] = jnp.concatenate(
            [even[:, width:], odd[:, width:]], axis=1
        )
    scores_ref[...] = jnp.dot(
        flat[...].astype(jnp.bfloat16), turned[...], preferred_element_type=jnp.float32
    )

    for copy in side_copies + mix_copies:
        copy.wait_send()
    await_bytes(pick_in, pick_sems.at[0])
    await_bytes(stat_in, stat_sems.at[0])
    await_bytes(grad_in.at[pl.ds(0, count - 1)], grad_sems.at[0])


def class_rows(tokens):
    short = tokens // 10 // 16 * 16
    return tokens // 2 - short, short


def per_device_any(count, parts, hidden, head_weight, in_proj, out_proj, targets, lengths, grad_store):
    tokens, block = hidden.shape
    vocab_cols = head_weight.shape[1]
    width = in_proj.shape[1]
    own = tokens // count
    tiles = tokens // TILE
    fits = (
        count % (4 * parts) == 0
        and block % LANES == 0
        and 2 * width == LANES
        and own % 32 == 0
        and tokens % 32 == 0
        and tokens >= 160
        and TILE % own == 0
        and grad_store.shape[1] == width * width
        and width * width % (4 * LANES) == 0
        and vocab_cols % (2 * LANES) == 0
    )
    if not fits:
        return per_device(hidden, head_weight, in_proj, out_proj, targets, lengths, grad_store)
    line = count // 4
    seq_count = lengths.shape[0]
    hbm = pl.BlockSpec(memory_space=pltpu.HBM)
    vmem = pl.BlockSpec(memory_space=pltpu.VMEM)
    dma = pltpu.SemaphoreType.DMA
    f32, bf16 = jnp.float32, jnp.bfloat16
    return pl.pallas_call(
        functools.partial(kernel, line, parts),
        out_shape=jax.ShapeDtypeStruct((seq_count, grad_store.shape[0]), f32),
        in_specs=[hbm] * 7,
        out_specs=vmem,
        scratch_shapes=[
            pltpu.VMEM((count, tokens, block), bf16),
            pltpu.VMEM((head_weight.shape[0] * parts, vocab_cols), bf16),
            pltpu.VMEM((tokens, vocab_cols), f32),
            pltpu.VMEM((tokens, width), f32),
            pltpu.VMEM(grad_store.shape, bf16),
            pltpu.VMEM(grad_store.shape[::-1], bf16),
            pltpu.VMEM(in_proj.shape[::-1], bf16),
            pltpu.VMEM(out_proj.shape[::-1], bf16),
            pltpu.VMEM((1, tokens), jnp.int32),
            pltpu.SMEM(lengths.shape, jnp.int32),
            pltpu.VMEM((vocab_cols, LANES), bf16),
            pltpu.VMEM((tokens, LANES), bf16),
            pltpu.VMEM((count - 1, own, LANES), bf16),
            pltpu.VMEM((tokens, LANES), f32),
            pltpu.VMEM((count - 1, own, LANES), f32),
            pltpu.VMEM((own // 2, LANES), f32),
            pltpu.VMEM((count, own // 2, LANES), f32),
            pltpu.VMEM((parts, width, width), f32),
            pltpu.VMEM((parts, tiles, width, LANES), f32),
            pltpu.VMEM((parts, tiles, width, LANES), f32),
            pltpu.VMEM((seq_count * width, LANES), f32),
            pltpu.VMEM((seq_count, width * width), f32),
            dma((7,)),
            dma((parts, line)),
            dma((line,)),
            dma((4, 4, count)),
            dma((4, count)),
            dma((2,)),
            dma((2,)),
            dma((2,)),
            dma((parts,)),
            dma((parts,)),
            dma((parts,)),
            dma((parts,)),
        ],
        compiler_params=pltpu.CompilerParams(
            collective_id=0, has_side_effects=True, vmem_limit_bytes=64 * 1024 * 1024
        ),
        cost_estimate=pl.CostEstimate(
            flops=2 * tokens * block * count * vocab_cols,
            bytes_accessed=4 * tokens * block * count,
            transcendentals=tokens * vocab_cols,
        ),
    )(hidden, head_weight, in_proj.T, out_proj.T, targets[None, :], lengths, grad_store)


def solution(mesh):
    return jax.shard_map(
        functools.partial(per_device_any, mesh.shape["vocab"], mesh.shape["rows"]),
        mesh=mesh,
        in_specs=(
            P("rows", "vocab"),
            P("rows", "vocab"),
            P(),
            P("vocab", None),
            P("rows"),
            P(),
            P(("vocab", "rows"), None),
        ),
        out_specs=P(None, ("vocab", "rows")),
        check_vma=False,
    )
```

```python
import functools

import jax
import jax.numpy as jnp
from jax import lax
from jax.experimental import pallas as pl
from jax.experimental.pallas import tpu as pltpu
from jax.sharding import PartitionSpec as P

TILE = 128


damping_ratio = 0.1
tiny_value = 1e-06


def joined(value, axis, join):
    pieces = jax.tree.map(lambda part: lax.all_gather(part, axis), value)
    head = jax.tree.map(lambda part: part[0], pieces)
    tail = jax.tree.map(lambda part: part[1:], pieces)
    running, _ = lax.scan(lambda running, slab: (join(running, slab), None), head, tail)
    return running


def whiten(seq_grads, cov_out, cov_in):
    proj_width = cov_out.shape[0]
    seq_count = seq_grads.shape[0]
    identity = jnp.eye(proj_width, dtype=jnp.float32)
    damp_out = damping_ratio * jnp.trace(cov_out) / proj_width + tiny_value
    damp_in = damping_ratio * jnp.trace(cov_in) / proj_width + tiny_value
    lower_out = jnp.linalg.cholesky(cov_out + damp_out * identity)
    lower_in = jnp.linalg.cholesky(cov_in + damp_in * identity)
    stacked = jnp.transpose(seq_grads, (1, 0, 2)).reshape(proj_width, seq_count * proj_width)
    left_half = lax.linalg.triangular_solve(lower_out, stacked, left_side=True, lower=True)
    left_full = lax.linalg.triangular_solve(
        lower_out, left_half, left_side=True, lower=True, transpose_a=True
    )
    rows_form = jnp.transpose(
        left_full.reshape(proj_width, seq_count, proj_width), (1, 0, 2)
    ).reshape(seq_count * proj_width, proj_width)
    right_half = lax.linalg.triangular_solve(
        lower_in, rows_form, left_side=False, lower=True, transpose_a=True
    )
    right_full = lax.linalg.triangular_solve(lower_in, right_half, left_side=False, lower=True)
    return right_full.reshape(seq_count, proj_width * proj_width)


def combine_rows(earlier, later):
    max_one, sum_one, weight_one = earlier
    max_two, sum_two, weight_two = later
    joint_max = jnp.maximum(max_one, max_two)
    scale_one = jnp.exp(max_one - joint_max)
    scale_two = jnp.exp(max_two - joint_max)
    joint_sum = sum_one * scale_one + sum_two * scale_two
    joint_weight = weight_one * scale_one[:, None] + weight_two * scale_two[:, None]
    return (joint_max, joint_sum, joint_weight)


def per_device(hidden, head_weight, in_proj, out_proj, targets, lengths, grad_store):
    token_count = hidden.shape[0]
    vocab_cols = head_weight.shape[1]
    proj_width = in_proj.shape[1]
    tile_count = token_count // TILE
    features = lax.all_gather(hidden, "vocab", axis=1, tiled=True)
    out_table = out_proj.astype(jnp.float32)
    first_column = lax.axis_index("vocab") * vocab_cols
    column_ids = lax.broadcasted_iota(jnp.int32, (token_count, vocab_cols), 1) + first_column
    onehot = (column_ids == targets[:, None]).astype(jnp.float32)
    picked_local = jnp.dot(onehot, out_table, precision=lax.Precision.HIGHEST)
    picked = lax.psum(picked_local, "vocab")
    logits = jnp.dot(
        features,
        lax.all_gather(head_weight, "rows", axis=0, tiled=True),
        preferred_element_type=jnp.float32,
    )
    local_max = jnp.max(logits, axis=1)
    exponent = jnp.exp(logits - local_max[:, None])
    weighted = jnp.dot(exponent, out_table, precision=lax.Precision.HIGHEST)
    merged = joined((local_max, jnp.sum(exponent, axis=1), weighted), "vocab", combine_rows)
    out_grad = merged[2] / merged[1][:, None] - picked
    input_proj = jnp.dot(features, in_proj, preferred_element_type=jnp.float32)
    own_lengths = lax.dynamic_slice_in_dim(lengths, lax.axis_index("rows") * tile_count, tile_count)
    position = lax.broadcasted_iota(jnp.int32, (tile_count, TILE), 1)
    is_valid = (position < own_lengths[:, None]).astype(jnp.float32)[:, :, None]
    out_tiles = out_grad.reshape(tile_count, TILE, proj_width) * is_valid
    in_tiles = input_proj.reshape(tile_count, TILE, proj_width) * is_valid
    flat_out = out_tiles.reshape(token_count, proj_width)
    flat_in = in_tiles.reshape(token_count, proj_width)
    local_out = jnp.dot(flat_out.T, flat_out, precision=lax.Precision.HIGHEST)
    local_in = jnp.dot(flat_in.T, flat_in, precision=lax.Precision.HIGHEST)
    cov_out, cov_in = lax.psum((local_out, local_in), "rows")
    row_total = jnp.sum(lengths).astype(jnp.float32)
    seq_grads = jnp.einsum("stk,stj->skj", out_tiles, in_tiles, precision=lax.Precision.HIGHEST)
    seq_grads = seq_grads / jnp.sqrt(own_lengths.astype(jnp.float32))[:, None, None]
    whitened = whiten(seq_grads, cov_out / row_total, cov_in / row_total).astype(jnp.bfloat16)
    return jnp.dot(
        lax.all_gather(whitened, "rows", axis=0, tiled=True),
        grad_store.T,
        preferred_element_type=jnp.float32,
    )


LANES = 128
HIGHEST = lax.Precision.HIGHEST
MESH = pl.DeviceIdType.MESH


def dot_f32(left, right, dims):
    return lax.dot_general(
        left, right, (dims, ((), ())), precision=HIGHEST, preferred_element_type=jnp.float32
    )


def split(value):
    upper = value.astype(jnp.bfloat16)
    return upper, (value - upper.astype(jnp.float32)).astype(jnp.bfloat16)


def dot_three(left, right):
    left_upper, left_lower = split(left)
    right_upper, right_lower = split(right)
    small = jnp.dot(left_upper, right_lower, preferred_element_type=jnp.float32) + jnp.dot(
        left_lower, right_upper, preferred_element_type=jnp.float32
    )
    return small + jnp.dot(left_upper, right_upper, preferred_element_type=jnp.float32)


def damped_inverse(cov):
    width = cov.shape[0]
    identity = (
        lax.broadcasted_iota(jnp.int32, cov.shape, 0) == lax.broadcasted_iota(jnp.int32, cov.shape, 1)
    ).astype(jnp.float32)
    diagonal = jnp.sum(cov * identity, axis=0, keepdims=True)
    trace = jnp.sum(diagonal, axis=1, keepdims=True)
    damp = damping_ratio * trace / width + tiny_value
    shrink = 1.0 / (damp + 0.5 * trace)
    scaled = (cov + identity * damp) * shrink
    reach = 1.0 / (1.0 + 2.0 * damping_ratio / width)
    gain = 2.0 / (2.0 - reach * reach)
    error = identity - scaled
    inverse = gain * (identity + error)
    error = (1.0 - gain) * identity + gain * dot_f32(error, error, ((1,), (0,)))
    reach = reach * reach / (2.0 - reach * reach)
    while reach > 1e-8:
        gain = 2.0 / (2.0 - reach * reach)
        reach = reach * reach / (2.0 - reach * reach)
        if reach > 1e-8:
            inverse = gain * (inverse + dot_f32(inverse, error, ((1,), (0,))))
            error = (1.0 - gain) * identity + gain * dot_f32(error, error, ((1,), (0,)))
        else:
            again = dot_f32(scaled, inverse, ((1,), (0,)))
            inverse = gain * (2.0 * inverse - dot_f32(inverse, again, ((1,), (0,))))
    return inverse * shrink


def kernel(
    line,
    parts,
    hidden_ref,
    head_ref,
    in_proj_hbm,
    out_proj_hbm,
    targets_hbm,
    lengths_hbm,
    store_ref,
    scores_ref,
    feat,
    weights,
    logits,
    inner,
    store,
    turned,
    in_proj_ref,
    out_proj_ref,
    targets_ref,
    lengths_ref,
    table,
    pick,
    pick_in,
    stat,
    stat_in,
    grad,
    grad_in,
    side_in,
    mix,
    mix_in,
    white,
    flat,
    load_sem,
    head_send,
    head_recv,
    feat_send,
    feat_recv,
    pick_sems,
    stat_sems,
    grad_sems,
    side_send,
    side_recv,
    mix_send,
    mix_recv,
):
    count = line * 4
    me = lax.axis_index("vocab")
    row = lax.axis_index("rows")
    z, y, x = me // 4, (me // 2) % 2, me % 2
    tokens, block = hidden_ref.shape
    long_rows, short_rows = class_rows(tokens)
    starts = (0, long_rows, 2 * long_rows, 2 * long_rows + short_rows)
    sizes = (long_rows, long_rows, short_rows, short_rows)
    depth, vocab_cols = head_ref.shape
    width = out_proj_ref.shape[0]
    own = tokens // count
    tiles = tokens // TILE
    seq_count = tiles * parts

    def send(source, target, send_sem, recv_sem, device):
        return pltpu.make_async_remote_copy(
            src_ref=source,
            dst_ref=target,
            send_sem=send_sem,
            recv_sem=recv_sem,
            device_id=device,
            device_id_type=MESH,
        )

    def await_bytes(ref, sem):
        pltpu.make_async_copy(ref, ref, sem).wait()

    barrier = pltpu.get_barrier_semaphore()

    def greet(step, carry):
        pl.semaphore_signal(
            barrier, inc=1, device_id={"vocab": (me + step) % count}, device_id_type=MESH
        )
        return carry

    lax.fori_loop(1, count, greet, 0)
    for step in range(1, parts):
        pl.semaphore_signal(
            barrier, inc=1, device_id={"rows": (row + step) % parts}, device_id_type=MESH
        )
    local_feat = pltpu.make_async_copy(hidden_ref, feat.at[me], load_sem.at[0])
    local_store = pltpu.make_async_copy(store_ref, store, load_sem.at[2])
    local_feat.start()
    small = [
        pltpu.make_async_copy(source, target, load_sem.at[3 + at])
        for at, (source, target) in enumerate(
            [
                (out_proj_hbm, out_proj_ref),
                (targets_hbm, targets_ref),
                (lengths_hbm, lengths_ref),
                (in_proj_hbm, in_proj_ref),
            ]
        )
    ]
    for copy in small:
        copy.start()
    chunk = 4 * block
    per_part = line // parts

    def head_chunk(zz):
        return weights.at[pl.ds(pl.multiple_of(zz * chunk, chunk), chunk)]

    for at in range(per_part):
        pltpu.make_async_copy(
            head_ref.at[pl.ds(at * chunk, chunk)],
            head_chunk(row * per_part + at),
            head_recv.at[row * per_part + at],
        ).start()
    local_store.start()
    pl.semaphore_wait(barrier, count - 1 + parts - 1)

    def place(zz, yy, xx):
        return (zz * 2 + yy) * 2 + xx

    def item(zz, side, pair):
        near, far = pair % 2, pair // 2
        flip_y, flip_x = (far, near) if side % 2 == 0 else (near, far)
        return place(zz, (y + flip_y) % 2, (x + flip_x) % 2)

    def piece(index, side):
        return feat.at[index, pl.ds(starts[side], sizes[side])]

    def hop(index, side, route, device, source=None):
        return send(
            piece(index, side) if source is None else source,
            piece(index, side),
            feat_send.at[route, side, index],
            feat_recv.at[side, index],
            {"vocab": device},
        )

    nearest = jnp.minimum(z, line - 1 - z)

    def nth(k):
        if k == 0:
            return z
        sign_near = -1 if k % 2 == 1 else 1
        sign_far = jnp.where(z < line - 1 - z, 1, -1)
        return z + jnp.where(k <= 2 * nearest, sign_near * ((k + 1) // 2), sign_far * (k - nearest))

    def own_rows_of(side):
        return hidden_ref.at[pl.ds(starts[side], sizes[side])]

    def along(k, side, pair, action, source=None):
        zz = nth(k)
        index = item(zz, side, pair)
        up = z < line - 1
        down = z > 0
        if k > 0:
            up = jnp.logical_and(zz < z, up)
            down = jnp.logical_and(zz > z, down)

        @pl.when(up)
        def _():
            action(hop(index, side, 0, place(jnp.minimum(z + 1, line - 1), y, x), source))

        @pl.when(down)
        def _():
            action(hop(index, side, 1, place(jnp.maximum(z - 1, 0), y, x), source))

    def outward(k, side, action):
        source = own_rows_of(side) if k == 0 else None
        index = item(nth(k), side, 0)
        along(k, side, 0, action, source)
        action(hop(index, side, 2, item(z, side, 1), source))
        action(hop(index, side, 3, item(z, side, 2), source))

    def onward(k, side):
        return hop(item(nth(k), side, 1), side, 2, item(z, side, 2))

    def arrived(index, side):
        hop(index, side, 0, me).wait_recv()

    strip = 2 * LANES

    def multiply(k):
        zz = nth(k)
        for pair in (2, 3):
            for side in range(2):
                arrived(item(zz, side, pair), side)
        pltpu.make_async_copy(head_chunk(zz), head_chunk(zz), head_recv.at[zz]).wait()

        def wide():
            return jnp.concatenate([feat[place(zz, at // 2, at % 2)] for at in range(4)], axis=1)

        rows = pl.ds(pl.multiple_of(zz * chunk, chunk), chunk)

        def body(step, carry):
            columns = pl.ds(pl.multiple_of(step * strip, strip), strip)
            product = jnp.dot(wide(), weights[rows, columns], preferred_element_type=jnp.float32)
            logits[:, columns] = product if k == 0 else logits[:, columns] + product
            return carry

        lax.fori_loop(0, vocab_cols // strip, body, 0)
        product = lax.dot_general(
            wide(), in_proj_ref[:, rows], (((1,), (1,)), ((), ())), preferred_element_type=jnp.float32
        )
        inner[...] = product if k == 0 else inner[...] + product

    def short_arrivals(k):
        for pair in range(4):
            for side in (2, 3):
                if k > 0:
                    arrived(item(nth(k), side, pair), side)
                    along(k, side, pair, lambda copy: copy.start())

    def short_start(side, action):
        source = own_rows_of(side)
        action(hop(me, side, 2, item(z, side, 1), source))
        action(hop(me, side, 3, item(z, side, 2), source))
        along(0, side, 0, action, source)

    def short_onward(pair, side, action):
        index = item(z, side, pair)
        if pair == 1:
            action(hop(index, side, 2, item(z, side, 2)))
        along(0, side, pair, action)

    for side in (2, 3):
        short_start(side, lambda copy: copy.start())
    for side in range(2):
        outward(0, side, lambda copy: copy.start())
    def head_copy(k, step):
        zz = nth(k)
        at = zz % per_part
        return send(
            head_ref.at[pl.ds(pl.multiple_of(at * chunk, chunk), chunk)],
            head_chunk(zz),
            head_send.at[step, zz],
            head_recv.at[zz],
            {"rows": (row + step) % parts},
        )

    def head_sends(action):
        for k in range(line):

            @pl.when(nth(k) // per_part == row)
            def _():
                for step in range(1, parts):
                    action(head_copy(k, step))

    head_sends(lambda copy: copy.start())

    def own_part(ref, device):
        return ref.at[pl.ds(pl.multiple_of(device * own, own), own)]

    def slot(device):
        return (me - device - 1 + 2 * count) % count

    def send_targets():
        for copy in small:
            copy.wait()
        marker = lax.broadcasted_iota(jnp.int32, (LANES - width, vocab_cols), 0)
        upright = jnp.concatenate([out_proj_ref[...].astype(jnp.float32), (marker == 0).astype(jnp.float32)], axis=0)
        table[...] = upright.T.astype(jnp.bfloat16)
        column_ids = lax.broadcasted_iota(jnp.int32, (vocab_cols, tokens), 0) + me * vocab_cols
        onehot = (column_ids == targets_ref[...]).astype(jnp.float32).astype(jnp.bfloat16)
        pick[...] = jnp.dot(
            upright.astype(jnp.bfloat16), onehot, preferred_element_type=jnp.float32
        ).T.astype(jnp.bfloat16)

        def send_pick(step, carry):
            device = (me + step) % count
            send(
                own_part(pick, device),
                pick_in.at[slot(device)],
                pick_sems.at[0],
                pick_sems.at[1],
                {"vocab": device},
            ).start()
            return carry

        lax.fori_loop(1, count, send_pick, 0)

    def turn_store():
        local_store.wait()
        turned_columns = 4 * LANES

        def turn(step, carry):
            columns = pl.ds(pl.multiple_of(step * turned_columns, turned_columns), turned_columns)
            turned[columns, :] = store[:, columns].astype(jnp.float32).T.astype(jnp.bfloat16)
            return carry

        lax.fori_loop(0, width * width // turned_columns, turn, 0)

    for pair in (1, 2, 3):
        for side in (2, 3):
            arrived(item(z, side, pair), side)
            short_onward(pair, side, lambda copy: copy.start())
    for k in range(1, line):
        for side in range(2):
            arrived(place(nth(k), y, x), side)
            outward(k, side, lambda copy: copy.start())
        for side in range(2):
            arrived(item(nth(k - 1), side, 1), side)
            onward(k - 1, side).start()
        if k > 1:
            short_arrivals(k - 1)
        if k == 1:
            send_targets()
            local_feat.wait()
        if k == line - 1:
            turn_store()
        if k > 1:
            multiply(k - 2)
    for side in range(2):
        arrived(item(nth(line - 1), side, 1), side)
        onward(line - 1, side).start()
    short_arrivals(line - 1)
    multiply(line - 2)
    multiply(line - 1)

    lanes = lax.broadcasted_iota(jnp.int32, (TILE, LANES), 1)
    per_tile = TILE // own
    for tile in range(tiles):
        part = logits[tile * TILE : (tile + 1) * TILE, :]
        top = jnp.max(part, axis=1, keepdims=True)
        exponent = jnp.exp(part - top)
        upper = exponent.astype(jnp.bfloat16)
        lower = (exponent - upper.astype(jnp.float32)).astype(jnp.bfloat16)
        weighted = jnp.dot(upper, table[...], preferred_element_type=jnp.float32) + jnp.dot(
            lower, table[...], preferred_element_type=jnp.float32
        )
        stat[tile * TILE : (tile + 1) * TILE, :] = jnp.where(lanes == width + 1, top, weighted)
        for device in range(tile * per_tile, (tile + 1) * per_tile):

            @pl.when(me != device)
            def _():
                send(
                    stat.at[pl.ds(device * own, own)],
                    stat_in.at[slot(device)],
                    stat_sems.at[0],
                    stat_sems.at[1],
                    {"vocab": device},
                ).start()

    position = lax.broadcasted_iota(jnp.int32, (TILE, LANES), 0)
    masked_in = []
    for tile in range(tiles):
        valid = (position < lengths_ref[row * tiles + tile]).astype(jnp.float32)
        masked_in.append(inner[tile * TILE : (tile + 1) * TILE, :] * valid[:, :width])
    flat_in = jnp.concatenate(masked_in, axis=0)
    side_in[row] = dot_f32(flat_in, flat_in, ((0,), (0,)))
    side_copies = []
    for step in range(1, parts):
        copy = send(
            side_in.at[row], side_in.at[row], side_send.at[step], side_recv.at[row], {"rows": (row + step) % parts}
        )
        copy.start()
        side_copies.append(copy)
    row_total = lengths_ref[0]
    for sequence in range(1, seq_count):
        row_total = row_total + lengths_ref[sequence]
    one_over = 1.0 / jnp.full((1, width), row_total, jnp.int32).astype(jnp.float32)
    for k in range(line):
        for side in range(2):
            outward(k, side, lambda copy: copy.wait_send())
            onward(k, side).wait_send()
        for side in (2, 3):
            for pair in range(4):
                if k > 0:
                    along(k, side, pair, lambda copy: copy.wait_send())
                elif pair > 0:
                    short_onward(pair, side, lambda copy: copy.wait_send())
                else:
                    short_start(side, lambda copy: copy.wait_send())
    head_sends(lambda copy: copy.wait_send())
    for step in range(1, parts):
        other = (row + step) % parts
        send(side_in.at[row], side_in.at[other], side_send.at[0], side_recv.at[other], {"rows": row}).wait_recv()
    cov_in = side_in[0]
    for part in range(1, parts):
        cov_in = cov_in + side_in[part]
    inverse_in = damped_inverse(cov_in * one_over)
    flat_in = dot_three(flat_in, inverse_in)

    await_bytes(pick_in, pick_sems.at[1])
    picked = own_part(pick, me)[...].astype(jnp.float32)
    for other in range(count - 1):
        picked = picked + pick_in[other].astype(jnp.float32)
    await_bytes(stat_in, stat_sems.at[1])
    mine = own_part(stat, me)[...]
    tops = [mine[:, width + 1 : width + 2]]
    for other in range(count - 1):
        tops.append(stat_in[other][:, width + 1 : width + 2])
    joint = functools.reduce(jnp.maximum, tops)
    total = mine * jnp.exp(tops[0] - joint)
    for other in range(count - 1):
        total = total + stat_in[other] * jnp.exp(tops[other + 1] - joint)
    first = me * own
    place_in_tile = lax.broadcasted_iota(jnp.int32, (own, LANES), 0) + first % TILE
    valid = (place_in_tile < lengths_ref[row * tiles + first // TILE]).astype(jnp.float32)
    finished = (total / total[:, width : width + 1] - picked) * valid
    grad[...] = jnp.concatenate([finished[: own // 2, :width], finished[own // 2 :, :width]], axis=1)

    def send_grad(step, carry):
        device = (me + step) % count
        send(grad, grad_in.at[me], grad_sems.at[0], grad_sems.at[1], {"vocab": device}).start()
        return carry

    lax.fori_loop(1, count, send_grad, 0)
    grad_in[me] = grad[...]
    await_bytes(grad_in.at[pl.ds(0, count - 1)], grad_sems.at[1])

    for tile in range(tiles):
        pieces = []
        for other in range(tile * per_tile, (tile + 1) * per_tile):
            pieces += [grad_in[other][:, :width], grad_in[other][:, width:]]
        grads = jnp.concatenate(pieces, axis=0)
        joined_sides = jnp.concatenate([grads, flat_in[tile * TILE : (tile + 1) * TILE, :]], axis=1)
        mix[row, tile] = dot_f32(grads, joined_sides, ((0,), (0,)))
    mix_copies = []
    for step in range(1, parts):
        copy = send(
            mix.at[row], mix_in.at[row], mix_send.at[step], mix_recv.at[row], {"rows": (row + step) % parts}
        )
        copy.start()
        mix_copies.append(copy)
    mix_in[row] = mix[row]
    for step in range(1, parts):
        other = (row + step) % parts
        send(mix.at[row], mix_in.at[other], mix_send.at[0], mix_recv.at[other], {"rows": row}).wait_recv()

    cov_out = jnp.zeros((width, LANES), jnp.float32)
    stacked = []
    for part in range(parts):
        for tile in range(tiles):
            block_mix = mix_in[part, tile]
            cov_out = cov_out + block_mix
            long = jnp.full((1, LANES), lengths_ref[part * tiles + tile], jnp.int32)
            stacked.append(block_mix * lax.rsqrt(long.astype(jnp.float32)))
    inverse_out = damped_inverse(cov_out[:, :width] * one_over)
    whitened = dot_three(inverse_out, jnp.concatenate(stacked, axis=1))
    for sequence in range(seq_count):
        white[sequence * width : (sequence + 1) * width, :] = whitened[
            :, sequence * LANES : (sequence + 1) * LANES
        ]
    for pair in range(width // 2):
        even = white[pl.ds(2 * pair, seq_count, stride=width), :]
        odd = white[pl.ds(2 * pair + 1, seq_count, stride=width), :]
        flat[:, pair * LANES : (pair + 1) * LANES] = jnp.concatenate(
            [even[:, width:], odd[:, width:]], axis=1
        )
    scores_ref[...] = jnp.dot(
        flat[...].astype(jnp.bfloat16), turned[...], preferred_element_type=jnp.float32
    )

    for copy in side_copies + mix_copies:
        copy.wait_send()
    await_bytes(pick_in, pick_sems.at[0])
    await_bytes(stat_in, stat_sems.at[0])
    await_bytes(grad_in.at[pl.ds(0, count - 1)], grad_sems.at[0])


def class_rows(tokens):
    short = tokens // 10 // 16 * 16
    return tokens // 2 - short, short


def per_device_any(count, parts, hidden, head_weight, in_proj, out_proj, targets, lengths, grad_store):
    tokens, block = hidden.shape
    vocab_cols = head_weight.shape[1]
    width = in_proj.shape[1]
    own = tokens // count
    tiles = tokens // TILE
    fits = (
        count % (4 * parts) == 0
        and count > 4
        and block % LANES == 0
        and 2 * width == LANES
        and own % 32 == 0
        and tokens % 32 == 0
        and tokens >= 160
        and TILE % own == 0
        and grad_store.shape[1] == width * width
        and width * width % (4 * LANES) == 0
        and vocab_cols % (2 * LANES) == 0
    )
    if not fits:
        return per_device(hidden, head_weight, in_proj, out_proj, targets, lengths, grad_store)
    line = count // 4
    seq_count = lengths.shape[0]
    hbm = pl.BlockSpec(memory_space=pltpu.HBM)
    vmem = pl.BlockSpec(memory_space=pltpu.VMEM)
    dma = pltpu.SemaphoreType.DMA
    f32, bf16 = jnp.float32, jnp.bfloat16
    return pl.pallas_call(
        functools.partial(kernel, line, parts),
        out_shape=jax.ShapeDtypeStruct((seq_count, grad_store.shape[0]), f32),
        in_specs=[hbm] * 7,
        out_specs=vmem,
        scratch_shapes=[
            pltpu.VMEM((count, tokens, block), bf16),
            pltpu.VMEM((head_weight.shape[0] * parts, vocab_cols), bf16),
            pltpu.VMEM((tokens, vocab_cols), f32),
            pltpu.VMEM((tokens, width), f32),
            pltpu.VMEM(grad_store.shape, bf16),
            pltpu.VMEM(grad_store.shape[::-1], bf16),
            pltpu.VMEM(in_proj.shape[::-1], bf16),
            pltpu.VMEM(out_proj.shape[::-1], bf16),
            pltpu.VMEM((1, tokens), jnp.int32),
            pltpu.SMEM(lengths.shape, jnp.int32),
            pltpu.VMEM((vocab_cols, LANES), bf16),
            pltpu.VMEM((tokens, LANES), bf16),
            pltpu.VMEM((count - 1, own, LANES), bf16),
            pltpu.VMEM((tokens, LANES), f32),
            pltpu.VMEM((count - 1, own, LANES), f32),
            pltpu.VMEM((own // 2, LANES), f32),
            pltpu.VMEM((count, own // 2, LANES), f32),
            pltpu.VMEM((parts, width, width), f32),
            pltpu.VMEM((parts, tiles, width, LANES), f32),
            pltpu.VMEM((parts, tiles, width, LANES), f32),
            pltpu.VMEM((seq_count * width, LANES), f32),
            pltpu.VMEM((seq_count, width * width), f32),
            dma((7,)),
            dma((parts, line)),
            dma((line,)),
            dma((4, 4, count)),
            dma((4, count)),
            dma((2,)),
            dma((2,)),
            dma((2,)),
            dma((parts,)),
            dma((parts,)),
            dma((parts,)),
            dma((parts,)),
        ],
        compiler_params=pltpu.CompilerParams(
            collective_id=0, has_side_effects=True, vmem_limit_bytes=64 * 1024 * 1024
        ),
        cost_estimate=pl.CostEstimate(
            flops=2 * tokens * block * count * vocab_cols,
            bytes_accessed=4 * tokens * block * count,
            transcendentals=tokens * vocab_cols,
        ),
    )(hidden, head_weight, in_proj.T, out_proj.T, targets[None, :], lengths, grad_store)


def solution(mesh):
    return jax.shard_map(
        functools.partial(per_device_any, mesh.shape["vocab"], mesh.shape["rows"]),
        mesh=mesh,
        in_specs=(
            P("rows", "vocab"),
            P("rows", "vocab"),
            P(),
            P("vocab", None),
            P("rows"),
            P(),
            P(("vocab", "rows"), None),
        ),
        out_specs=P(None, ("vocab", "rows")),
        check_vma=False,
    )
```

```python
import functools

import jax
import jax.numpy as jnp
from jax import lax
from jax.experimental import pallas as pl
from jax.experimental.pallas import tpu as pltpu
from jax.sharding import PartitionSpec as P

TILE = 128


damping_ratio = 0.1
tiny_value = 1e-06


def joined(value, axis, join):
    pieces = jax.tree.map(lambda part: lax.all_gather(part, axis), value)
    head = jax.tree.map(lambda part: part[0], pieces)
    tail = jax.tree.map(lambda part: part[1:], pieces)
    running, _ = lax.scan(lambda running, slab: (join(running, slab), None), head, tail)
    return running


def whiten(seq_grads, cov_out, cov_in):
    proj_width = cov_out.shape[0]
    seq_count = seq_grads.shape[0]
    identity = jnp.eye(proj_width, dtype=jnp.float32)
    damp_out = damping_ratio * jnp.trace(cov_out) / proj_width + tiny_value
    damp_in = damping_ratio * jnp.trace(cov_in) / proj_width + tiny_value
    lower_out = jnp.linalg.cholesky(cov_out + damp_out * identity)
    lower_in = jnp.linalg.cholesky(cov_in + damp_in * identity)
    stacked = jnp.transpose(seq_grads, (1, 0, 2)).reshape(proj_width, seq_count * proj_width)
    left_half = lax.linalg.triangular_solve(lower_out, stacked, left_side=True, lower=True)
    left_full = lax.linalg.triangular_solve(
        lower_out, left_half, left_side=True, lower=True, transpose_a=True
    )
    rows_form = jnp.transpose(
        left_full.reshape(proj_width, seq_count, proj_width), (1, 0, 2)
    ).reshape(seq_count * proj_width, proj_width)
    right_half = lax.linalg.triangular_solve(
        lower_in, rows_form, left_side=False, lower=True, transpose_a=True
    )
    right_full = lax.linalg.triangular_solve(lower_in, right_half, left_side=False, lower=True)
    return right_full.reshape(seq_count, proj_width * proj_width)


def combine_rows(earlier, later):
    max_one, sum_one, weight_one = earlier
    max_two, sum_two, weight_two = later
    joint_max = jnp.maximum(max_one, max_two)
    scale_one = jnp.exp(max_one - joint_max)
    scale_two = jnp.exp(max_two - joint_max)
    joint_sum = sum_one * scale_one + sum_two * scale_two
    joint_weight = weight_one * scale_one[:, None] + weight_two * scale_two[:, None]
    return (joint_max, joint_sum, joint_weight)


def per_device(hidden, head_weight, in_proj, out_proj, targets, lengths, grad_store):
    token_count = hidden.shape[0]
    vocab_cols = head_weight.shape[1]
    proj_width = in_proj.shape[1]
    tile_count = token_count // TILE
    features = lax.all_gather(hidden, "vocab", axis=1, tiled=True)
    out_table = out_proj.astype(jnp.float32)
    first_column = lax.axis_index("vocab") * vocab_cols
    column_ids = lax.broadcasted_iota(jnp.int32, (token_count, vocab_cols), 1) + first_column
    onehot = (column_ids == targets[:, None]).astype(jnp.float32)
    picked_local = jnp.dot(onehot, out_table, precision=lax.Precision.HIGHEST)
    picked = lax.psum(picked_local, "vocab")
    logits = jnp.dot(
        features,
        lax.all_gather(head_weight, "rows", axis=0, tiled=True),
        preferred_element_type=jnp.float32,
    )
    local_max = jnp.max(logits, axis=1)
    exponent = jnp.exp(logits - local_max[:, None])
    weighted = jnp.dot(exponent, out_table, precision=lax.Precision.HIGHEST)
    merged = joined((local_max, jnp.sum(exponent, axis=1), weighted), "vocab", combine_rows)
    out_grad = merged[2] / merged[1][:, None] - picked
    input_proj = jnp.dot(features, in_proj, preferred_element_type=jnp.float32)
    own_lengths = lax.dynamic_slice_in_dim(lengths, lax.axis_index("rows") * tile_count, tile_count)
    position = lax.broadcasted_iota(jnp.int32, (tile_count, TILE), 1)
    is_valid = (position < own_lengths[:, None]).astype(jnp.float32)[:, :, None]
    out_tiles = out_grad.reshape(tile_count, TILE, proj_width) * is_valid
    in_tiles = input_proj.reshape(tile_count, TILE, proj_width) * is_valid
    flat_out = out_tiles.reshape(token_count, proj_width)
    flat_in = in_tiles.reshape(token_count, proj_width)
    local_out = jnp.dot(flat_out.T, flat_out, precision=lax.Precision.HIGHEST)
    local_in = jnp.dot(flat_in.T, flat_in, precision=lax.Precision.HIGHEST)
    cov_out, cov_in = lax.psum((local_out, local_in), "rows")
    row_total = jnp.sum(lengths).astype(jnp.float32)
    seq_grads = jnp.einsum("stk,stj->skj", out_tiles, in_tiles, precision=lax.Precision.HIGHEST)
    seq_grads = seq_grads / jnp.sqrt(own_lengths.astype(jnp.float32))[:, None, None]
    whitened = whiten(seq_grads, cov_out / row_total, cov_in / row_total).astype(jnp.bfloat16)
    return jnp.dot(
        lax.all_gather(whitened, "rows", axis=0, tiled=True),
        grad_store.T,
        preferred_element_type=jnp.float32,
    )


LANES = 128
HIGHEST = lax.Precision.HIGHEST
MESH = pl.DeviceIdType.MESH


def dot_f32(left, right, dims):
    return lax.dot_general(
        left, right, (dims, ((), ())), precision=HIGHEST, preferred_element_type=jnp.float32
    )


def split(value):
    upper = value.astype(jnp.bfloat16)
    return upper, (value - upper.astype(jnp.float32)).astype(jnp.bfloat16)


def dot_three(left, right):
    left_upper, left_lower = split(left)
    right_upper, right_lower = split(right)
    small = jnp.dot(left_upper, right_lower, preferred_element_type=jnp.float32) + jnp.dot(
        left_lower, right_upper, preferred_element_type=jnp.float32
    )
    return small + jnp.dot(left_upper, right_upper, preferred_element_type=jnp.float32)


def damped_inverse(cov):
    width = cov.shape[0]
    identity = (
        lax.broadcasted_iota(jnp.int32, cov.shape, 0) == lax.broadcasted_iota(jnp.int32, cov.shape, 1)
    ).astype(jnp.float32)
    diagonal = jnp.sum(cov * identity, axis=0, keepdims=True)
    trace = jnp.sum(diagonal, axis=1, keepdims=True)
    damp = damping_ratio * trace / width + tiny_value
    shrink = 1.0 / (damp + 0.5 * trace)
    scaled = (cov + identity * damp) * shrink
    reach = 1.0 / (1.0 + 2.0 * damping_ratio / width)
    gain = 2.0 / (2.0 - reach * reach)
    error = identity - scaled
    inverse = gain * (identity + error)
    error = (1.0 - gain) * identity + gain * dot_three(error, error)
    reach = reach * reach / (2.0 - reach * reach)
    while reach > 1e-8:
        gain = 2.0 / (2.0 - reach * reach)
        reach = reach * reach / (2.0 - reach * reach)
        if reach > 1e-8:
            inverse = gain * (inverse + dot_three(inverse, error))
            error = (1.0 - gain) * identity + gain * dot_three(error, error)
        else:
            again = dot_f32(scaled, inverse, ((1,), (0,)))
            inverse = gain * (2.0 * inverse - dot_f32(inverse, again, ((1,), (0,))))
    return inverse * shrink


def kernel(
    line,
    parts,
    hidden_ref,
    head_ref,
    in_proj_hbm,
    out_proj_hbm,
    targets_hbm,
    lengths_hbm,
    store_ref,
    scores_ref,
    feat,
    weights,
    logits,
    inner,
    store,
    turned,
    in_proj_ref,
    out_proj_ref,
    targets_ref,
    lengths_ref,
    table,
    pick,
    pick_in,
    stat,
    stat_in,
    grad,
    grad_in,
    side_in,
    mix,
    mix_in,
    white,
    flat,
    load_sem,
    head_send,
    head_recv,
    feat_send,
    feat_recv,
    pick_sems,
    stat_sems,
    grad_sems,
    side_send,
    side_recv,
    mix_send,
    mix_recv,
):
    count = line * 4
    me = lax.axis_index("vocab")
    row = lax.axis_index("rows")
    z, y, x = me // 4, (me // 2) % 2, me % 2
    tokens, block = hidden_ref.shape
    long_rows, short_rows = class_rows(tokens)
    starts = (0, long_rows, 2 * long_rows, 2 * long_rows + short_rows)
    sizes = (long_rows, long_rows, short_rows, short_rows)
    depth, vocab_cols = head_ref.shape
    width = out_proj_ref.shape[0]
    own = tokens // count
    tiles = tokens // TILE
    seq_count = tiles * parts

    def send(source, target, send_sem, recv_sem, device):
        return pltpu.make_async_remote_copy(
            src_ref=source,
            dst_ref=target,
            send_sem=send_sem,
            recv_sem=recv_sem,
            device_id=device,
            device_id_type=MESH,
        )

    def await_bytes(ref, sem):
        pltpu.make_async_copy(ref, ref, sem).wait()

    barrier = pltpu.get_barrier_semaphore()

    def greet(step, carry):
        pl.semaphore_signal(
            barrier, inc=1, device_id={"vocab": (me + step) % count}, device_id_type=MESH
        )
        return carry

    lax.fori_loop(1, count, greet, 0)
    for step in range(1, parts):
        pl.semaphore_signal(
            barrier, inc=1, device_id={"rows": (row + step) % parts}, device_id_type=MESH
        )
    local_feat = pltpu.make_async_copy(hidden_ref, feat.at[me], load_sem.at[0])
    local_store = pltpu.make_async_copy(store_ref, store, load_sem.at[2])
    local_feat.start()
    small = [
        pltpu.make_async_copy(source, target, load_sem.at[3 + at])
        for at, (source, target) in enumerate(
            [
                (out_proj_hbm, out_proj_ref),
                (targets_hbm, targets_ref),
                (lengths_hbm, lengths_ref),
                (in_proj_hbm, in_proj_ref),
            ]
        )
    ]
    for copy in small:
        copy.start()
    chunk = 4 * block
    per_part = line // parts

    def head_chunk(zz):
        return weights.at[pl.ds(pl.multiple_of(zz * chunk, chunk), chunk)]

    for at in range(per_part):
        pltpu.make_async_copy(
            head_ref.at[pl.ds(at * chunk, chunk)],
            head_chunk(row * per_part + at),
            head_recv.at[row * per_part + at],
        ).start()
    local_store.start()
    pl.semaphore_wait(barrier, count - 1 + parts - 1)

    def place(zz, yy, xx):
        return (zz * 2 + yy) * 2 + xx

    def item(zz, side, pair):
        near, far = pair % 2, pair // 2
        flip_y, flip_x = (far, near) if side % 2 == 0 else (near, far)
        return place(zz, (y + flip_y) % 2, (x + flip_x) % 2)

    def piece(index, side):
        return feat.at[index, pl.ds(starts[side], sizes[side])]

    def hop(index, side, route, device, source=None):
        return send(
            piece(index, side) if source is None else source,
            piece(index, side),
            feat_send.at[route, side, index],
            feat_recv.at[side, index],
            {"vocab": device},
        )

    nearest = jnp.minimum(z, line - 1 - z)

    def nth(k):
        if k == 0:
            return z
        sign_near = -1 if k % 2 == 1 else 1
        sign_far = jnp.where(z < line - 1 - z, 1, -1)
        return z + jnp.where(k <= 2 * nearest, sign_near * ((k + 1) // 2), sign_far * (k - nearest))

    def own_rows_of(side):
        return hidden_ref.at[pl.ds(starts[side], sizes[side])]

    def along(k, side, pair, action, source=None):
        zz = nth(k)
        index = item(zz, side, pair)
        up = z < line - 1
        down = z > 0
        if k > 0:
            up = jnp.logical_and(zz < z, up)
            down = jnp.logical_and(zz > z, down)

        @pl.when(up)
        def _():
            action(hop(index, side, 0, place(jnp.minimum(z + 1, line - 1), y, x), source))

        @pl.when(down)
        def _():
            action(hop(index, side, 1, place(jnp.maximum(z - 1, 0), y, x), source))

    def outward(k, side, action):
        source = own_rows_of(side) if k == 0 else None
        index = item(nth(k), side, 0)
        along(k, side, 0, action, source)
        action(hop(index, side, 2, item(z, side, 1), source))
        action(hop(index, side, 3, item(z, side, 2), source))

    def onward(k, side):
        return hop(item(nth(k), side, 1), side, 2, item(z, side, 2))

    def arrived(index, side):
        hop(index, side, 0, me).wait_recv()

    strip = 4 * LANES

    def multiply(k):
        zz = nth(k)
        for pair in (2, 3):
            for side in range(2):
                arrived(item(zz, side, pair), side)
        pltpu.make_async_copy(head_chunk(zz), head_chunk(zz), head_recv.at[zz]).wait()

        def wide():
            return jnp.concatenate([feat[place(zz, at // 2, at % 2)] for at in range(4)], axis=1)

        rows = pl.ds(pl.multiple_of(zz * chunk, chunk), chunk)

        def body(step, carry):
            columns = pl.ds(pl.multiple_of(step * strip, strip), strip)
            product = jnp.dot(wide(), weights[rows, columns], preferred_element_type=jnp.float32)
            logits[:, columns] = product if k == 0 else logits[:, columns] + product
            return carry

        lax.fori_loop(0, vocab_cols // strip, body, 0)
        product = lax.dot_general(
            wide(), in_proj_ref[:, rows], (((1,), (1,)), ((), ())), preferred_element_type=jnp.float32
        )
        inner[...] = product if k == 0 else inner[...] + product

    def short_arrivals(k):
        for pair in range(4):
            for side in (2, 3):
                if k > 0:
                    arrived(item(nth(k), side, pair), side)
                    along(k, side, pair, lambda copy: copy.start())

    def short_start(side, action):
        source = own_rows_of(side)
        action(hop(me, side, 2, item(z, side, 1), source))
        action(hop(me, side, 3, item(z, side, 2), source))
        along(0, side, 0, action, source)

    def short_onward(pair, side, action):
        index = item(z, side, pair)
        if pair == 1:
            action(hop(index, side, 2, item(z, side, 2)))
        along(0, side, pair, action)

    for side in (2, 3):
        short_start(side, lambda copy: copy.start())
    for side in range(2):
        outward(0, side, lambda copy: copy.start())
    def head_copy(k, step):
        zz = nth(k)
        at = zz % per_part
        return send(
            head_ref.at[pl.ds(pl.multiple_of(at * chunk, chunk), chunk)],
            head_chunk(zz),
            head_send.at[step, zz],
            head_recv.at[zz],
            {"rows": (row + step) % parts},
        )

    def head_sends(action):
        for k in range(line):

            @pl.when(nth(k) // per_part == row)
            def _():
                for step in range(1, parts):
                    action(head_copy(k, step))

    head_sends(lambda copy: copy.start())

    def own_part(ref, device):
        return ref.at[pl.ds(pl.multiple_of(device * own, own), own)]

    def slot(device):
        return (me - device - 1 + 2 * count) % count

    def send_targets():
        for copy in small:
            copy.wait()
        marker = lax.broadcasted_iota(jnp.int32, (LANES - width, vocab_cols), 0)
        upright = jnp.concatenate([out_proj_ref[...].astype(jnp.float32), (marker == 0).astype(jnp.float32)], axis=0)
        table[...] = upright.T.astype(jnp.bfloat16)
        column_ids = lax.broadcasted_iota(jnp.int32, (vocab_cols, tokens), 0) + me * vocab_cols
        onehot = (column_ids == targets_ref[...]).astype(jnp.float32).astype(jnp.bfloat16)
        pick[...] = jnp.dot(
            upright.astype(jnp.bfloat16), onehot, preferred_element_type=jnp.float32
        ).T.astype(jnp.bfloat16)

        def send_pick(step, carry):
            device = (me + step) % count
            send(
                own_part(pick, device),
                pick_in.at[slot(device)],
                pick_sems.at[0],
                pick_sems.at[1],
                {"vocab": device},
            ).start()
            return carry

        lax.fori_loop(1, count, send_pick, 0)

    def turn_store():
        local_store.wait()
        turned_columns = 4 * LANES

        def turn(step, carry):
            columns = pl.ds(pl.multiple_of(step * turned_columns, turned_columns), turned_columns)
            turned[columns, :] = store[:, columns].astype(jnp.float32).T.astype(jnp.bfloat16)
            return carry

        lax.fori_loop(0, width * width // turned_columns, turn, 0)

    for pair in (1, 2, 3):
        for side in (2, 3):
            arrived(item(z, side, pair), side)
            short_onward(pair, side, lambda copy: copy.start())
    for k in range(1, line):
        for side in range(2):
            arrived(place(nth(k), y, x), side)
            outward(k, side, lambda copy: copy.start())
        for side in range(2):
            arrived(item(nth(k - 1), side, 1), side)
            onward(k - 1, side).start()
        if k > 1:
            short_arrivals(k - 1)
        if k == 1:
            send_targets()
            local_feat.wait()
        if k == line - 1:
            turn_store()
        if k > 1:
            multiply(k - 2)
    for side in range(2):
        arrived(item(nth(line - 1), side, 1), side)
        onward(line - 1, side).start()
    short_arrivals(line - 1)
    multiply(line - 2)
    multiply(line - 1)

    lanes = lax.broadcasted_iota(jnp.int32, (TILE, LANES), 1)
    per_tile = TILE // own
    for tile in range(tiles):
        part = logits[tile * TILE : (tile + 1) * TILE, :]
        top = jnp.max(part, axis=1, keepdims=True)
        exponent = jnp.exp(part - top)
        upper = exponent.astype(jnp.bfloat16)
        lower = (exponent - upper.astype(jnp.float32)).astype(jnp.bfloat16)
        weighted = jnp.dot(upper, table[...], preferred_element_type=jnp.float32) + jnp.dot(
            lower, table[...], preferred_element_type=jnp.float32
        )
        stat[tile * TILE : (tile + 1) * TILE, :] = jnp.where(lanes == width + 1, top, weighted)
        for device in range(tile * per_tile, (tile + 1) * per_tile):

            @pl.when(me != device)
            def _():
                send(
                    stat.at[pl.ds(device * own, own)],
                    stat_in.at[slot(device)],
                    stat_sems.at[0],
                    stat_sems.at[1],
                    {"vocab": device},
                ).start()

    position = lax.broadcasted_iota(jnp.int32, (TILE, LANES), 0)
    masked_in = []
    for tile in range(tiles):
        valid = (position < lengths_ref[row * tiles + tile]).astype(jnp.float32)
        masked_in.append(inner[tile * TILE : (tile + 1) * TILE, :] * valid[:, :width])
    flat_in = jnp.concatenate(masked_in, axis=0)
    side_in[row] = dot_f32(flat_in, flat_in, ((0,), (0,)))
    side_copies = []
    for step in range(1, parts):
        copy = send(
            side_in.at[row], side_in.at[row], side_send.at[step], side_recv.at[row], {"rows": (row + step) % parts}
        )
        copy.start()
        side_copies.append(copy)
    row_total = lengths_ref[0]
    for sequence in range(1, seq_count):
        row_total = row_total + lengths_ref[sequence]
    one_over = 1.0 / jnp.full((1, width), row_total, jnp.int32).astype(jnp.float32)
    for k in range(line):
        for side in range(2):
            outward(k, side, lambda copy: copy.wait_send())
            onward(k, side).wait_send()
        for side in (2, 3):
            for pair in range(4):
                if k > 0:
                    along(k, side, pair, lambda copy: copy.wait_send())
                elif pair > 0:
                    short_onward(pair, side, lambda copy: copy.wait_send())
                else:
                    short_start(side, lambda copy: copy.wait_send())
    head_sends(lambda copy: copy.wait_send())
    for step in range(1, parts):
        other = (row + step) % parts
        send(side_in.at[row], side_in.at[other], side_send.at[0], side_recv.at[other], {"rows": row}).wait_recv()
    cov_in = side_in[0]
    for part in range(1, parts):
        cov_in = cov_in + side_in[part]
    inverse_in = damped_inverse(cov_in * one_over)
    flat_in = dot_three(flat_in, inverse_in)

    await_bytes(pick_in, pick_sems.at[1])
    picked = own_part(pick, me)[...].astype(jnp.float32)
    for other in range(count - 1):
        picked = picked + pick_in[other].astype(jnp.float32)
    await_bytes(stat_in, stat_sems.at[1])
    mine = own_part(stat, me)[...]
    tops = [mine[:, width + 1 : width + 2]]
    for other in range(count - 1):
        tops.append(stat_in[other][:, width + 1 : width + 2])
    joint = functools.reduce(jnp.maximum, tops)
    total = mine * jnp.exp(tops[0] - joint)
    for other in range(count - 1):
        total = total + stat_in[other] * jnp.exp(tops[other + 1] - joint)
    first = me * own
    place_in_tile = lax.broadcasted_iota(jnp.int32, (own, LANES), 0) + first % TILE
    valid = (place_in_tile < lengths_ref[row * tiles + first // TILE]).astype(jnp.float32)
    finished = (total / total[:, width : width + 1] - picked) * valid
    grad[...] = jnp.concatenate([finished[: own // 2, :width], finished[own // 2 :, :width]], axis=1)

    def send_grad(step, carry):
        device = (me + step) % count
        send(grad, grad_in.at[me], grad_sems.at[0], grad_sems.at[1], {"vocab": device}).start()
        return carry

    lax.fori_loop(1, count, send_grad, 0)
    grad_in[me] = grad[...]
    await_bytes(grad_in.at[pl.ds(0, count - 1)], grad_sems.at[1])

    for tile in range(tiles):
        pieces = []
        for other in range(tile * per_tile, (tile + 1) * per_tile):
            pieces += [grad_in[other][:, :width], grad_in[other][:, width:]]
        grads = jnp.concatenate(pieces, axis=0)
        joined_sides = jnp.concatenate([grads, flat_in[tile * TILE : (tile + 1) * TILE, :]], axis=1)
        mix[row, tile] = dot_f32(grads, joined_sides, ((0,), (0,)))
    mix_copies = []
    for step in range(1, parts):
        copy = send(
            mix.at[row], mix_in.at[row], mix_send.at[step], mix_recv.at[row], {"rows": (row + step) % parts}
        )
        copy.start()
        mix_copies.append(copy)
    mix_in[row] = mix[row]
    for step in range(1, parts):
        other = (row + step) % parts
        send(mix.at[row], mix_in.at[other], mix_send.at[0], mix_recv.at[other], {"rows": row}).wait_recv()

    cov_out = jnp.zeros((width, LANES), jnp.float32)
    stacked = []
    for part in range(parts):
        for tile in range(tiles):
            block_mix = mix_in[part, tile]
            cov_out = cov_out + block_mix
            long = jnp.full((1, LANES), lengths_ref[part * tiles + tile], jnp.int32)
            stacked.append(block_mix * lax.rsqrt(long.astype(jnp.float32)))
    inverse_out = damped_inverse(cov_out[:, :width] * one_over)
    whitened = dot_three(inverse_out, jnp.concatenate(stacked, axis=1))
    for sequence in range(seq_count):
        white[sequence * width : (sequence + 1) * width, :] = whitened[
            :, sequence * LANES : (sequence + 1) * LANES
        ]
    for pair in range(width // 2):
        even = white[pl.ds(2 * pair, seq_count, stride=width), :]
        odd = white[pl.ds(2 * pair + 1, seq_count, stride=width), :]
        flat[:, pair * LANES : (pair + 1) * LANES] = jnp.concatenate(
            [even[:, width:], odd[:, width:]], axis=1
        )
    scores_ref[...] = jnp.dot(
        flat[...].astype(jnp.bfloat16), turned[...], preferred_element_type=jnp.float32
    )

    for copy in side_copies + mix_copies:
        copy.wait_send()
    await_bytes(pick_in, pick_sems.at[0])
    await_bytes(stat_in, stat_sems.at[0])
    await_bytes(grad_in.at[pl.ds(0, count - 1)], grad_sems.at[0])


def class_rows(tokens):
    short = tokens // 10 // 16 * 16
    return tokens // 2 - short, short


def per_device_any(count, parts, hidden, head_weight, in_proj, out_proj, targets, lengths, grad_store):
    tokens, block = hidden.shape
    vocab_cols = head_weight.shape[1]
    width = in_proj.shape[1]
    own = tokens // count
    tiles = tokens // TILE
    fits = (
        count % (4 * parts) == 0
        and count > 4
        and block % LANES == 0
        and 2 * width == LANES
        and own % 32 == 0
        and tokens % 32 == 0
        and tokens >= 160
        and TILE % own == 0
        and grad_store.shape[1] == width * width
        and width * width % (4 * LANES) == 0
        and vocab_cols % (4 * LANES) == 0
    )
    if not fits:
        return per_device(hidden, head_weight, in_proj, out_proj, targets, lengths, grad_store)
    line = count // 4
    seq_count = lengths.shape[0]
    hbm = pl.BlockSpec(memory_space=pltpu.HBM)
    vmem = pl.BlockSpec(memory_space=pltpu.VMEM)
    dma = pltpu.SemaphoreType.DMA
    f32, bf16 = jnp.float32, jnp.bfloat16
    return pl.pallas_call(
        functools.partial(kernel, line, parts),
        out_shape=jax.ShapeDtypeStruct((seq_count, grad_store.shape[0]), f32),
        in_specs=[hbm] * 7,
        out_specs=vmem,
        scratch_shapes=[
            pltpu.VMEM((count, tokens, block), bf16),
            pltpu.VMEM((head_weight.shape[0] * parts, vocab_cols), bf16),
            pltpu.VMEM((tokens, vocab_cols), f32),
            pltpu.VMEM((tokens, width), f32),
            pltpu.VMEM(grad_store.shape, bf16),
            pltpu.VMEM(grad_store.shape[::-1], bf16),
            pltpu.VMEM(in_proj.shape[::-1], bf16),
            pltpu.VMEM(out_proj.shape[::-1], bf16),
            pltpu.VMEM((1, tokens), jnp.int32),
            pltpu.SMEM(lengths.shape, jnp.int32),
            pltpu.VMEM((vocab_cols, LANES), bf16),
            pltpu.VMEM((tokens, LANES), bf16),
            pltpu.VMEM((count - 1, own, LANES), bf16),
            pltpu.VMEM((tokens, LANES), f32),
            pltpu.VMEM((count - 1, own, LANES), f32),
            pltpu.VMEM((own // 2, LANES), f32),
            pltpu.VMEM((count, own // 2, LANES), f32),
            pltpu.VMEM((parts, width, width), f32),
            pltpu.VMEM((parts, tiles, width, LANES), f32),
            pltpu.VMEM((parts, tiles, width, LANES), f32),
            pltpu.VMEM((seq_count * width, LANES), f32),
            pltpu.VMEM((seq_count, width * width), f32),
            dma((7,)),
            dma((parts, line)),
            dma((line,)),
            dma((4, 4, count)),
            dma((4, count)),
            dma((2,)),
            dma((2,)),
            dma((2,)),
            dma((parts,)),
            dma((parts,)),
            dma((parts,)),
            dma((parts,)),
        ],
        compiler_params=pltpu.CompilerParams(
            collective_id=0, has_side_effects=True, vmem_limit_bytes=64 * 1024 * 1024
        ),
        cost_estimate=pl.CostEstimate(
            flops=2 * tokens * block * count * vocab_cols,
            bytes_accessed=4 * tokens * block * count,
            transcendentals=tokens * vocab_cols,
        ),
    )(hidden, head_weight, in_proj.T, out_proj.T, targets[None, :], lengths, grad_store)


def solution(mesh):
    return jax.shard_map(
        functools.partial(per_device_any, mesh.shape["vocab"], mesh.shape["rows"]),
        mesh=mesh,
        in_specs=(
            P("rows", "vocab"),
            P("rows", "vocab"),
            P(),
            P("vocab", None),
            P("rows"),
            P(),
            P(("vocab", "rows"), None),
        ),
        out_specs=P(None, ("vocab", "rows")),
        check_vma=False,
    )
```
